512 devices in a mesh: rep: 64 (over y, z_lo, x), fsdp: 8 (over z_hi, core).
Axes of the slice: x: 4, y: 4, z: 16 (z_hi: 4, z_lo: 4; z = z_hi * 4 + z_lo), core: 2. Of those that a mesh axis runs over, the one named last changes fastest.
Arguments:
- activations: bfloat16 [64, 1536, 5120], P('rep', 'fsdp'), may hold values from -6 to 6
- doc_ids: int32 [64, 1536], P('rep', 'fsdp'), may hold values from 0 to 15, never falling along the last dimension, each value on 1 to 192 neighbouring positions
- step_index: int32 [1], replicated, may hold values from 0 to 63
- proj_weights: bfloat16 [64, 5120, 384], P('rep', 'fsdp'), may hold values from -1 to 1
- first_moment: bfloat16 [64, 5120, 384], P('rep', 'fsdp'), may hold values from -12 to 12
- second_moment: bfloat16 [64, 5120, 384], P('rep', 'fsdp'), may hold values from 0.0099487305 to 100
- out_grad: bfloat16 [64, 1536, 128], P('rep', 'fsdp'), may hold values from -6 to 6
Outputs:
- mixed_weights: bfloat16 [64, 5120, 384], P('rep', 'fsdp')
- first_next: bfloat16 [64, 5120, 384], P('rep', 'fsdp')
- second_next: bfloat16 [64, 5120, 384], P('rep', 'fsdp')
The draws below stay inside these ranges and needn't reach their ends.
All inputs are finite; a program needn't handle non-finite values.
Results may differ from the reference program's by a relative error of at most 0.035.
Values may be sent and summed in bfloat16 or wider, within the bound.
A program may use at most 64 MiB of HBM per device.

```python
import math
import jax
import jax.numpy as jnp
import numpy as np
from jax import lax

D = 5120
HD = 128
SEQ = 192
TOK = 1536
REPLICAS = 64
N_REP = 64


def draw_activations(key, part):
    key = jax.random.fold_in(key, 11)
    noise = jax.random.truncated_normal(key, -6.0, 6.0, (REPLICAS, TOK, D), jnp.float32)
    return noise.astype(jnp.bfloat16)


def draw_proj_weights(key, part):
    key = jax.random.fold_in(key, 23)
    noise_key = jax.random.fold_in(key, 0)
    base = jax.random.truncated_normal(noise_key, -4.0, 4.0, (REPLICAS, D, 3 * HD), jnp.float32) / math.sqrt(D)
    return base.astype(jnp.bfloat16)


def steps_of(stream_key, extent, cuts, smallest, largest):
    def one(dim, shards_of):
        draws = jax.random.uniform(jax.random.fold_in(jax.random.fold_in(stream_key, 6), dim), (shards_of,), jnp.float32, smallest / len(cuts), largest / len(cuts))
        return jnp.repeat(jnp.exp(draws), extent[dim] // shards_of).reshape((-1,) + (1,) * (len(extent) - dim - 1))

    gain = one(*cuts[0])
    for cut in cuts[1:]:
        gain = gain * one(*cut)
    return gain


def split_up(amount, total, limit, lean):
    loads = [(1 << 20) // math.isqrt(standing ** lean) + 1 for standing in range(2, amount + 1)]
    surplus, given = total - limit - (amount - 1), [1] * (amount - 1)
    while surplus > 0:
        free = [i for i in range(amount - 1) if given[i] < limit]
        mass, left = sum([loads[i] for i in free]), surplus
        for i in free:
            addition = min(limit - given[i], max(1, left * loads[i] // mass), surplus)
            given[i] = given[i] + addition
            surplus = surplus - addition
    return np.array([limit] + given)


def ragged_sizes(rng, amount, total, bound, lean):
    if amount == 2:
        one = jax.random.randint(rng, (), max(1, total - bound), min(bound, total - 1) + 1)
        return jnp.stack([one, total - one])
    sizes = jnp.asarray(split_up(amount, total, bound, lean), jnp.int32)
    twos = (amount - 1) // 2
    source_of, receiver = sizes[1:1 + 2 * twos:2], sizes[2:2 + 2 * twos:2]
    margin = jnp.minimum(source_of - 1, bound - receiver)
    moved = jax.random.randint(jax.random.fold_in(rng, 1), (twos,), 0, 1 << 20) % (margin + 1)
    sizes = sizes.at[1:1 + 2 * twos:2].set(source_of - moved).at[2:2 + 2 * twos:2].set(receiver + moved)
    return sizes[jax.random.permutation(jax.random.fold_in(rng, 2), amount)]


def normal_values(stream_key, shape, deviation, most, cuts=(), kind=jnp.bfloat16):
    array = deviation * jax.random.normal(stream_key, shape, jnp.float32)
    if cuts:
        array = array * steps_of(stream_key, shape, cuts, -0.22, 0.18)
    return jnp.clip(array, -most, most).astype(kind)


def setup_inputs(seed: int = 0) -> dict:
    arg_keys = jax.random.split(jax.random.key(seed), 8)
    return {
        "activations": draw_activations(jax.random.fold_in(arg_keys[7], 71), 0),
        "doc_ids": jax.vmap(lambda own: jnp.searchsorted(jnp.cumsum(ragged_sizes(own, 2 * TOK // SEQ, TOK, SEQ, 0)), jnp.arange(TOK), side="right"))(jax.random.split(arg_keys[1], REPLICAS)).reshape((REPLICAS, TOK)).astype(jnp.int32),
        "step_index": jax.random.randint(arg_keys[2], (1,), 0, 64).astype(jnp.int32),
        "proj_weights": draw_proj_weights(jax.random.fold_in(arg_keys[7], 71), 0),
        "first_moment": normal_values(arg_keys[4], (REPLICAS, D, 3 * HD), 2.0, 12.0, ((0, 64), (1, 8))),
        "second_moment": jnp.clip(jnp.exp(math.log(100.0) - 9.215481 * jax.random.uniform(arg_keys[5], (REPLICAS, D, 3 * HD), jnp.float32) ** steps_of(arg_keys[5], (REPLICAS, D, 3 * HD), ((0, 64), (1, 8)), -0.2, 0.2)), 0.0099487305, 100.0).astype(jnp.bfloat16),
        "out_grad": normal_values(arg_keys[6], (REPLICAS, TOK, HD), 1.0, 6.0, ((0, 64), (1, 8))),
    }


BETA_ONE = 0.9
BETA_TWO = 0.95
LEARN_RATE = 0.002
DECAY_RATE = 0.1
ADAM_EPS = 1e-08

def rms_rows(activ_rows):
    values = activ_rows.astype(jnp.float32)
    scale = lax.rsqrt(lax.optimization_barrier(jnp.mean(values * values, axis=-1, keepdims=True)) + 1e-05)
    return (values * scale).astype(jnp.bfloat16)

def rotate(block, cosine_tab, sine_tab):
    half = block.shape[1] // 2
    first = block[:, :half]
    second = block[:, half:]
    return jnp.concatenate([first * cosine_tab - second * sine_tab, first * sine_tab + second * cosine_tab], axis=1)

def attend(projected, doc_row):
    length = projected.shape[0]
    head_dim = projected.shape[1] // 3
    query = projected[:, :head_dim]
    keys = projected[:, head_dim:2 * head_dim]
    values = projected[:, 2 * head_dim:]
    position = jnp.arange(length).astype(jnp.float32)
    inverse = 10000.0 ** (-(jnp.arange(head_dim // 2).astype(jnp.float32) * 2.0 / head_dim))
    angles = position[:, None] * inverse[None, :]
    cosine_tab = jnp.cos(angles)
    sine_tab = jnp.sin(angles)
    query = rotate(query, cosine_tab, sine_tab)
    keys = rotate(keys, cosine_tab, sine_tab)
    scores = jnp.dot(query, keys.T, precision=lax.Precision.HIGHEST) * head_dim ** (-0.5)
    places = jnp.arange(length)
    allowed = (places[None, :] <= places[:, None]) & (doc_row[:, None] == doc_row[None, :])
    scores = jnp.where(allowed, scores, -1e+30)
    row_max = lax.stop_gradient(lax.optimization_barrier(jnp.max(scores, axis=1, keepdims=True)))
    expo = jnp.exp(scores - row_max)
    probs = (expo / lax.optimization_barrier(jnp.sum(expo, axis=1, keepdims=True))).astype(jnp.bfloat16)
    return jnp.dot(probs, values.astype(jnp.bfloat16), preferred_element_type=jnp.float32)

def adam_update(shard, grad, first, second, step_index):
    count = (step_index[0] + 1).astype(jnp.float32)
    weights = shard.astype(jnp.float32)
    first_new = BETA_ONE * first.astype(jnp.float32) + (1.0 - BETA_ONE) * grad
    second_new = BETA_TWO * second.astype(jnp.float32) + (1.0 - BETA_TWO) * grad * grad
    first_hat = first_new / (1.0 - jnp.power(BETA_ONE, count))
    second_hat = second_new / (1.0 - jnp.power(BETA_TWO, count))
    updated = weights - LEARN_RATE * (first_hat / (jnp.sqrt(second_hat) + ADAM_EPS) + DECAY_RATE * weights)
    return (updated.astype(jnp.bfloat16), first_new.astype(jnp.bfloat16), second_new.astype(jnp.bfloat16))

def reference(activations, doc_ids, step_index, proj_weights, first_moment, second_moment, out_grad):
    seq_count = TOK // SEQ

    def replica_step(items):
        activ_rows, doc_row, shard, first, second, grad_rows = items
        normed = rms_rows(activ_rows)
        projected = jnp.dot(normed, shard, preferred_element_type=jnp.float32).astype(jnp.bfloat16)
        grouped = projected.reshape(seq_count, SEQ, -1)

        def backward(pieces):
            proj_seq, doc_seq, grad_seq = pieces
            result, pullback = jax.vjp(lambda inner: attend(inner, doc_seq), proj_seq.astype(jnp.float32))
            return pullback(grad_seq.astype(jnp.float32))[0].astype(jnp.bfloat16)
        proj_grad = lax.map(backward, (grouped, doc_row.reshape(seq_count, SEQ), grad_rows.reshape(seq_count, SEQ, -1)))

        def term(pieces):
            return lax.dot_general(pieces[0], pieces[1], (((0,), (0,)), ((), ())), preferred_element_type=jnp.float32)
        terms = lax.map(term, (normed.reshape(seq_count, SEQ, -1), proj_grad))
        rounded = lax.optimization_barrier(terms.astype(jnp.bfloat16))
        grad = lax.optimization_barrier(jnp.sum(rounded.astype(jnp.float32), axis=0))
        return adam_update(shard, grad, first, second, step_index)
    updated, first_next, second_next = lax.map(replica_step, (activations, doc_ids, proj_weights, first_moment, second_moment, out_grad))
    level = step_index[0] % (N_REP.bit_length() - 1)
    distance = jnp.left_shift(jnp.ones((), jnp.int32), level.astype(jnp.int32))
    partners = jnp.bitwise_xor(jnp.arange(N_REP).astype(jnp.int32), distance)
    partner_rows = jnp.take(updated, partners, axis=0)
    mixed_weights = ((updated.astype(jnp.float32) + partner_rows.astype(jnp.float32)) * 0.5).astype(jnp.bfloat16)
    return (mixed_weights, first_next, second_next)
```

```python
import functools

import jax
import jax.numpy as jnp
import numpy as np
from jax import lax
from jax.experimental import pallas as pl
from jax.experimental.pallas import tpu as pltpu
from jax.sharding import PartitionSpec as P

BETA_ONE = 0.9
BETA_TWO = 0.95
LEARN_RATE = 0.002
DECAY_RATE = 0.1
ADAM_EPS = 1e-08

MESH = pl.DeviceIdType.MESH
F32 = jnp.float32
BF16 = jnp.bfloat16
STAGES = 4


def rotary_tables(length, head_dim):
    position = np.arange(length, dtype=np.float32)
    inverse = np.float32(10000.0) ** (-(np.arange(head_dim // 2, dtype=np.float32) * np.float32(2.0 / head_dim)))
    angles = (position[:, None] * inverse[None, :]).astype(np.float32)
    cosine, sine = np.cos(angles), np.sin(angles)
    return np.concatenate([cosine, cosine, -sine, sine], axis=1).astype(np.float32)


def dot(a, b, contract, precision=None):
    return lax.dot_general(a, b, ((contract[0], contract[1]), ((), ())), precision=precision, preferred_element_type=F32)


def attention_grad(projected, doc_row, tables, out_grad):
    length, width = projected.shape
    hd = width // 3
    high = lax.Precision.HIGHEST
    cosine, sine = tables[:, :hd], tables[:, hd:]

    def rotate(x):
        return x * cosine + pltpu.roll(x, hd // 2, 1) * sine

    def rotate_back(x):
        return x * cosine - pltpu.roll(x, hd // 2, 1) * sine

    query = rotate(projected[:, :hd].astype(F32))
    keys = rotate(projected[:, hd : 2 * hd].astype(F32))
    values = projected[:, 2 * hd :]
    rows = lax.broadcasted_iota(jnp.int32, (length, length), 0)
    columns = lax.broadcasted_iota(jnp.int32, (length, length), 1)
    doc_wide = jnp.broadcast_to(doc_row.astype(F32), (length, length))
    doc_col = jnp.sum(jnp.where(rows == columns, doc_wide, 0.0), axis=1, keepdims=True)
    allowed = (columns <= rows) & (doc_wide == doc_col)
    scale = hd ** (-0.5)
    scores = dot(query, keys, ((1,), (1,)), high) * scale
    scores = jnp.where(allowed, scores, -1e30)
    expo = jnp.exp(scores - jnp.max(scores, axis=1, keepdims=True))
    probs = expo / jnp.sum(expo, axis=1, keepdims=True)
    probs_low = probs.astype(BF16)
    grad_values = dot(probs_low, out_grad, ((0,), (0,)))
    grad_probs = dot(out_grad, values, ((1,), (1,)))
    inner = jnp.sum(grad_probs * probs, axis=1, keepdims=True)
    grad_scores = probs * (grad_probs - inner) * scale
    grad_query = rotate_back(dot(grad_scores, keys, ((1,), (0,)), high))
    grad_keys = rotate_back(dot(grad_scores, query, ((0,), (0,)), high))
    return grad_query.astype(BF16), grad_keys.astype(BF16), grad_values.astype(BF16)


def kernel(
    bit, hops,
    coef_ref, doc_ref, tab_ref, act_hbm, w_hbm, first_hbm, second_hbm, og_hbm,
    mixed_hbm, first_out, second_out,
    act_v, xs, xsend, xt, wall, pacc, precv, g_ref, topp, tright, tleft, ropp_l, ropp_r, rleft, rright,
    first_v, second_v, og_v, upd, prt, mix_v, first_o, second_o,
    loc_sem, out_sem, ag_send, ag_recv, x_send, x_recv, p_send, p_recv,
    opp_send, opp_recv, rs_send, rs_recv, sw_send, sw_recv,
):
    rep = lax.axis_index("rep")
    own = lax.axis_index("fsdp")
    z, core = own // 2, own % 2
    right = (rep, ((z + 1) % hops) * 2 + core)
    left = (rep, ((z + hops - 1) % hops) * 2 + core)
    sibling = (rep, z * 2 + (1 - core))
    distance = 2**bit
    partner = (rep + (1 - 2 * ((rep // distance) % 2)) * distance, own)
    seq, width = act_v.shape
    depth, cols = wall.shape[1:]
    half = depth // 2
    chunk = half // STAGES

    def remote(src, dst, send, recv, device):
        return pltpu.make_async_remote_copy(
            src_ref=src, dst_ref=dst, send_sem=send, recv_sem=recv, device_id=device, device_id_type=MESH
        )

    load_act = pltpu.make_async_copy(act_hbm, act_v, loc_sem.at[0])
    load_w = pltpu.make_async_copy(w_hbm, wall.at[0], loc_sem.at[1])
    load_first = pltpu.make_async_copy(first_hbm, first_v, loc_sem.at[2])
    load_second = pltpu.make_async_copy(second_hbm, second_v, loc_sem.at[3])
    load_og = pltpu.make_async_copy(og_hbm, og_v, loc_sem.at[4])
    for load in (load_act, load_w, load_first, load_second, load_og):
        load.start()

    barrier = pltpu.get_barrier_semaphore()
    for device in (right, left, sibling, partner):
        pl.semaphore_signal(barrier, inc=1, device_id=device, device_id_type=MESH)
    pl.semaphore_wait(barrier, 4)

    upper, lower = pl.ds(0, half), pl.ds(half, half)
    gathers = [
        remote(w_hbm.at[upper], wall.at[3, upper], ag_send.at[0], ag_recv.at[0], right),
        remote(w_hbm.at[lower], wall.at[1, lower], ag_send.at[1], ag_recv.at[1], left),
        remote(w_hbm.at[lower], wall.at[3, lower], ag_send.at[2], ag_recv.at[2], right),
        remote(w_hbm.at[upper], wall.at[1, upper], ag_send.at[3], ag_recv.at[3], left),
    ]
    forwards = [
        remote(wall.at[3, upper], wall.at[2, upper], ag_send.at[4], ag_recv.at[4], right),
        remote(wall.at[1, lower], wall.at[2, lower], ag_send.at[5], ag_recv.at[5], left),
    ]
    for copy in gathers:
        copy.start()

    load_act.wait()
    step_rows = 32

    def norm_rows(i, carry):
        rows = pl.ds(pl.multiple_of(i * step_rows, step_rows), step_rows)
        values = act_v[rows, :].astype(F32)
        scale = lax.rsqrt(jnp.sum(values * values, axis=-1, keepdims=True) * (1.0 / width) + 1e-05)
        for d in range(hops):
            block = ((z + d) % hops) * 2
            mine = pl.ds(pl.multiple_of((block + core) * depth, 128), depth)
            other = pl.ds(pl.multiple_of((block + 1 - core) * depth, 128), depth)
            xs[d, rows, :] = (act_v[rows, mine].astype(F32) * scale).astype(BF16)
            xsend[d, rows, :] = (act_v[rows, other].astype(F32) * scale).astype(BF16)
        return carry

    lax.fori_loop(0, seq // step_rows, norm_rows, 0)
    trades = [
        remote(xsend.at[d], xs.at[d, pl.ds(seq, seq)], x_send.at[d], x_recv.at[d], sibling) for d in range(hops)
    ]
    for copy in trades:
        copy.start()
    for copy in trades:
        copy.wait()
    load_w.wait()

    def turn(d, carry):
        xt[d] = xs[d].T
        return carry

    lax.fori_loop(0, hops, turn, 0)

    pacc[...] = dot(xs[0], wall[0], ((1,), (0,)))
    gathers[0].wait_recv()
    forwards[0].start()
    gathers[1].wait_recv()
    forwards[1].start()
    gathers[2].wait_recv()
    pacc[...] += dot(xs[3], wall[3], ((1,), (0,)))
    gathers[3].wait_recv()
    pacc[...] += dot(xs[1], wall[1], ((1,), (0,)))
    for copy in forwards:
        copy.wait_recv()
    pacc[...] += dot(xs[2], wall[2], ((1,), (0,)))

    give = remote(pacc.at[pl.ds(seq, seq)], precv, p_send.at[0], p_recv.at[0], sibling)
    give.start()
    load_og.wait()
    give.wait_recv()
    projected = (pacc[:seq, :] + precv[...]).astype(BF16)
    grads = attention_grad(projected, doc_ref[...], tab_ref[...], og_v[...])
    hd = cols // 3
    for n, part in enumerate(grads):
        g_ref[:seq, n * hd : (n + 1) * hd] = part
    give_g = remote(g_ref.at[pl.ds(0, seq)], g_ref.at[pl.ds(seq, seq)], p_send.at[1], p_recv.at[1], sibling)
    give_g.start()
    give_g.wait_recv()

    def rows_of(i, low):
        return pl.ds(pl.multiple_of(i * chunk + low * half, 16), chunk)

    def part_of(i):
        return pl.ds(pl.multiple_of(i * chunk, 16), chunk)

    def term(d, rows):
        return dot(xt[d, rows, :], g_ref[...], ((1,), (0,)))

    def opp_copy(i, low):
        rows = rows_of(i, low)
        if low:
            return remote(topp.at[rows], ropp_r.at[part_of(i)], opp_send.at[1, i], opp_recv.at[1, i], left)
        return remote(topp.at[rows], ropp_l.at[part_of(i)], opp_send.at[0, i], opp_recv.at[0, i], right)

    def rs_copy(i, low, way):
        rows = rows_of(i, low)
        if way:
            return remote(tleft.at[rows], rright.at[rows], rs_send.at[1, low, i], rs_recv.at[1, low, i], left)
        return remote(tright.at[rows], rleft.at[rows], rs_send.at[0, low, i], rs_recv.at[0, low, i], right)

    def swap_copy(i, low):
        rows = rows_of(i, low)
        return remote(upd.at[rows], prt.at[rows], sw_send.at[low, i], sw_recv.at[low, i], partner)

    def out_copies(i, low):
        rows = rows_of(i, low)
        return [
            pltpu.make_async_copy(first_o.at[rows], first_out.at[rows], out_sem.at[0, low, i]),
            pltpu.make_async_copy(second_o.at[rows], second_out.at[rows], out_sem.at[1, low, i]),
        ]

    def mix_copy(i, low):
        rows = rows_of(i, low)
        return pltpu.make_async_copy(mix_v.at[rows], mixed_hbm.at[rows], out_sem.at[2, low, i])

    def send_opposite(i, carry):
        for low in (0, 1):
            rows = rows_of(i, low)
            topp[rows, :] = term(2, rows).astype(BF16)
            opp_copy(i, low).start()
        return carry

    lax.fori_loop(0, STAGES, send_opposite, 0)

    def send_near(i, carry):
        up, down = rows_of(i, 0), rows_of(i, 1)
        tright[down, :] = term(1, down).astype(BF16)
        rs_copy(i, 1, 0).start()
        tleft[up, :] = term(3, up).astype(BF16)
        rs_copy(i, 0, 1).start()
        opp_copy(i, 0).wait_recv()
        tright[up, :] = (term(1, up) + ropp_l[part_of(i), :].astype(F32)).astype(BF16)
        rs_copy(i, 0, 0).start()
        opp_copy(i, 1).wait_recv()
        tleft[down, :] = (term(3, down) + ropp_r[part_of(i), :].astype(F32)).astype(BF16)
        rs_copy(i, 1, 1).start()
        return carry

    lax.fori_loop(0, STAGES, send_near, 0)

    load_first.wait()
    load_second.wait()
    fix_one, fix_two = coef_ref[0], coef_ref[1]

    def update(i, carry):
        for low in (0, 1):
            rows = rows_of(i, low)
            grad = term(0, rows)
            rs_copy(i, low, 0).wait_recv()
            rs_copy(i, low, 1).wait_recv()
            grad = grad + rleft[rows, :].astype(F32) + rright[rows, :].astype(F32)
            weights = wall[0, rows, :].astype(F32)
            first_new = BETA_ONE * first_v[rows, :].astype(F32) + (1.0 - BETA_ONE) * grad
            second_new = BETA_TWO * second_v[rows, :].astype(F32) + (1.0 - BETA_TWO) * grad * grad
            first_hat = first_new / fix_one
            second_hat = second_new / fix_two
            updated = weights - LEARN_RATE * (first_hat / (jnp.sqrt(second_hat) + ADAM_EPS) + DECAY_RATE * weights)
            upd[rows, :] = updated.astype(BF16)
            swap_copy(i, low).start()
            first_o[rows, :] = first_new.astype(BF16)
            second_o[rows, :] = second_new.astype(BF16)
            for copy in out_copies(i, low):
                copy.start()
        return carry

    def mix(i, carry):
        for low in (0, 1):
            rows = rows_of(i, low)
            swap_copy(i, low).wait_recv()
            mix_v[rows, :] = ((upd[rows, :].astype(F32) + prt[rows, :].astype(F32)) * 0.5).astype(BF16)
            mix_copy(i, low).start()
        return carry

    def update_and_mix(i, carry):
        update(i, carry)
        return mix(i - 1, carry)

    update(0, 0)
    lax.fori_loop(1, STAGES, update_and_mix, 0)
    mix(STAGES - 1, 0)

    for copy in gathers + forwards:
        copy.wait_send()
    give.wait_send()
    give_g.wait_send()

    def finish(i, carry):
        for low in (0, 1):
            opp_copy(i, low).wait_send()
            rs_copy(i, low, 0).wait_send()
            rs_copy(i, low, 1).wait_send()
            swap_copy(i, low).wait_send()
            for copy in out_copies(i, low):
                copy.wait()
            mix_copy(i, low).wait()
        return carry

    lax.fori_loop(0, STAGES, finish, 0)


def per_device(activations, doc_ids, step_index, proj_weights, first_moment, second_moment, out_grad):
    hops = lax.axis_size("fsdp") // 2
    seq, width = activations.shape[1:]
    depth, cols = proj_weights.shape[1:]
    half = depth // 2
    count = (step_index[0] + 1).astype(F32)
    coef = jnp.stack([1.0 - jnp.power(BETA_ONE, count), 1.0 - jnp.power(BETA_TWO, count)])
    tables = jnp.asarray(rotary_tables(seq, cols // 3))
    dma, vmem = pltpu.SemaphoreType.DMA, pltpu.VMEM
    row_block = jax.ShapeDtypeStruct((depth, cols), BF16)

    def branch(bit):
        return pl.pallas_call(
            functools.partial(kernel, bit, hops),
            out_shape=(row_block, row_block, row_block),
            in_specs=[
                pl.BlockSpec(memory_space=pltpu.SMEM),
                pl.BlockSpec(memory_space=pltpu.VMEM),
                pl.BlockSpec(memory_space=pltpu.VMEM),
            ]
            + [pl.BlockSpec(memory_space=pl.ANY)] * 5,
            out_specs=(pl.BlockSpec(memory_space=pl.ANY),) * 3,
            scratch_shapes=[
                vmem((seq, width), BF16),
                vmem((hops, 2 * seq, depth), BF16),
                vmem((hops, seq, depth), BF16),
                vmem((hops, depth, 2 * seq), BF16),
                vmem((hops, depth, cols), BF16),
                vmem((2 * seq, cols), F32),
                vmem((seq, cols), F32),
                vmem((2 * seq, cols), BF16),
                vmem((depth, cols), BF16),
                vmem((depth, cols), BF16),
                vmem((depth, cols), BF16),
                vmem((half, cols), BF16),
                vmem((half, cols), BF16),
                vmem((depth, cols), BF16),
                vmem((depth, cols), BF16),
                vmem((depth, cols), BF16),
                vmem((depth, cols), BF16),
                vmem((seq, cols // 3), BF16),
                vmem((depth, cols), BF16),
                vmem((depth, cols), BF16),
                vmem((depth, cols), BF16),
                vmem((depth, cols), BF16),
                vmem((depth, cols), BF16),
                dma((5,)),
                dma((3, 2, STAGES)),
                dma((6,)),
                dma((6,)),
                dma((hops,)),
                dma((hops,)),
                dma((2,)),
                dma((2,)),
                dma((2, STAGES)),
                dma((2, STAGES)),
                dma((2, 2, STAGES)),
                dma((2, 2, STAGES)),
                dma((2, STAGES)),
                dma((2, STAGES)),
            ],
            compiler_params=pltpu.CompilerParams(
                collective_id=bit, has_side_effects=True, vmem_limit_bytes=40 * 2**20
            ),
        )

    bit_total = lax.axis_size("rep").bit_length() - 1
    outs = lax.switch(
        step_index[0] % bit_total,
        [branch(bit) for bit in range(bit_total)],
        coef, doc_ids, tables, activations[0], proj_weights[0], first_moment[0], second_moment[0], out_grad[0],
    )
    return tuple(out[None] for out in outs)


def solution(mesh):
    rows = P("rep", "fsdp", None)
    return jax.shard_map(
        per_device,
        mesh=mesh,
        in_specs=(rows, P("rep", "fsdp"), P(), rows, rows, rows, rows),
        out_specs=(rows, rows, rows),
        check_vma=False,
    )
```

```python
import functools

import jax
import jax.numpy as jnp
import numpy as np
from jax import lax
from jax.experimental import pallas as pl
from jax.experimental.pallas import tpu as pltpu
from jax.sharding import PartitionSpec as P

BETA_ONE = 0.9
BETA_TWO = 0.95
LEARN_RATE = 0.002
DECAY_RATE = 0.1
ADAM_EPS = 1e-08

MESH = pl.DeviceIdType.MESH
F32 = jnp.float32
BF16 = jnp.bfloat16
STAGES = 8
PIECES = 2
NORM_ROWS = 32
RUN = 4
PARITY_SHIFT = 1


def rotary_tables(length, head_dim):
    position = np.arange(length, dtype=np.float32)
    inverse = np.float32(10000.0) ** (-(np.arange(head_dim // 2, dtype=np.float32) * np.float32(2.0 / head_dim)))
    angles = (position[:, None] * inverse[None, :]).astype(np.float32)
    cosine, sine = np.cos(angles), np.sin(angles)
    return np.concatenate([cosine, cosine, -sine, sine], axis=1).astype(np.float32)


def dot(a, b, contract, precision=None):
    return lax.dot_general(a, b, ((contract[0], contract[1]), ((), ())), precision=precision, preferred_element_type=F32)


def attention_grad(projected, allowed, tables, out_grad):
    length, width = projected.shape
    hd = width // 3
    high = lax.Precision.HIGHEST
    cosine, sine = tables[:, :hd], tables[:, hd:]

    def rotate(x):
        return x * cosine + pltpu.roll(x, hd // 2, 1) * sine

    def rotate_back(x):
        return x * cosine - pltpu.roll(x, hd // 2, 1) * sine

    query = rotate(projected[:, :hd].astype(F32))
    keys = rotate(projected[:, hd : 2 * hd].astype(F32))
    values = projected[:, 2 * hd :]
    scale = hd ** (-0.5)
    scores = dot(query, keys, ((1,), (1,)), high) * scale
    scores = jnp.where(allowed, scores, -1e30)
    expo = jnp.exp(scores - jnp.max(scores, axis=1, keepdims=True))
    probs = expo / jnp.sum(expo, axis=1, keepdims=True)
    probs_low = probs.astype(BF16)
    grad_values = dot(probs_low, out_grad, ((0,), (0,)))
    grad_probs = dot(out_grad, values, ((1,), (1,)))
    inner = jnp.sum(grad_probs * probs, axis=1, keepdims=True)
    grad_scores = probs * (grad_probs - inner) * scale
    grad_query = rotate_back(dot(grad_scores, keys, ((1,), (0,)), high))
    grad_keys = rotate_back(dot(grad_scores, query, ((0,), (0,)), high))
    return grad_query.astype(BF16), grad_keys.astype(BF16), grad_values.astype(BF16)


def kernel(
    bit, hops,
    coef_ref, doc_ref, tab_ref, act_hbm, w_hbm, first_hbm, second_hbm, og_hbm,
    mixed_hbm, first_out, second_out,
    act_v, xkeep, xaway, skeep, saway, xt, wall, mask, pacc, part_own, part_pair, psend, pz, g_ref,
    tsend, trecv, first_v, second_v, og_v, upd, prt, mix_v, first_o, second_o,
    loc_sem, out_sem, w_sem, x_send, x_recv, p_send, p_recv, g_send, g_recv, rs_send, rs_recv, sw_send, sw_recv,
):
    rep = lax.axis_index("rep")
    own = lax.axis_index("fsdp")
    z, core = own // 2, own % 2
    parity = ((rep // RUN) % hops + PARITY_SHIFT) // 2 % 2
    step = 1 - 2 * ((z + parity) % 2)
    pair_z, next_z, far_z = (z + step + hops) % hops, (z - step + hops) % hops, (z + 2) % hops
    pair = (rep, pair_z * 2 + core)
    following = (rep, next_z * 2 + core)
    sibling = (rep, z * 2 + (1 - core))
    distance = 2**bit
    partner = (rep + (1 - 2 * ((rep // distance) % 2)) * distance, own)
    seq, width = act_v.shape
    depth, cols = wall.shape[1:]
    chunk = depth // STAGES
    hd = cols // 3

    def remote(src, dst, send, recv, device):
        return pltpu.make_async_remote_copy(
            src_ref=src, dst_ref=dst, send_sem=send, recv_sem=recv, device_id=device, device_id_type=MESH
        )

    load_act = pltpu.make_async_copy(act_hbm, act_v, loc_sem.at[0])
    load_w = pltpu.make_async_copy(w_hbm, wall.at[0], loc_sem.at[1])
    load_first = pltpu.make_async_copy(first_hbm, first_v, loc_sem.at[2])
    load_second = pltpu.make_async_copy(second_hbm, second_v, loc_sem.at[3])
    load_og = pltpu.make_async_copy(og_hbm, og_v, loc_sem.at[4])
    for load in (load_act, load_w, load_first, load_second, load_og):
        load.start()

    barrier = pltpu.get_barrier_semaphore()
    for device in (pair, following, sibling, partner):
        pl.semaphore_signal(barrier, inc=1, device_id=device, device_id_type=MESH)
    pl.semaphore_wait(barrier, 4)

    send_w = remote(w_hbm, wall.at[1], w_sem.at[0], w_sem.at[1], following)
    send_w.start()

    load_act.wait()
    piece = seq // PIECES

    def rows_at(base, c):
        return pl.ds(pl.multiple_of(base + c * piece, 16), piece)

    def trade_away(c):
        return remote(saway.at[:, rows_at(0, c)], xaway.at[:, rows_at(seq, c)], x_send.at[0, c], x_recv.at[0, c], sibling)

    def trade_keep(c):
        return remote(skeep.at[:, rows_at(0, c)], xkeep.at[:, rows_at(seq, c)], x_send.at[1, c], x_recv.at[1, c], sibling)

    def pair_own(c):
        return remote(xaway.at[:, rows_at(0, c)], xkeep.at[:, rows_at(2 * seq, c)], x_send.at[2, c], x_recv.at[2, c], pair)

    def pair_sibling(c):
        return remote(xaway.at[:, rows_at(seq, c)], xkeep.at[:, rows_at(3 * seq, c)], x_send.at[3, c], x_recv.at[3, c], pair)

    def norm_piece(c, carry):
        def norm_rows(i, inner):
            rows = pl.ds(pl.multiple_of(c * piece + i * NORM_ROWS, 16), NORM_ROWS)
            values = act_v[rows, :].astype(F32)
            scale = lax.rsqrt(jnp.sum(values * values, axis=-1, keepdims=True) * (1.0 / width) + 1e-05)
            for block_z, mine, other, slot in (
                (pair_z, xaway, saway, 0), (far_z, xaway, saway, 1), (z, xkeep, skeep, 0), (next_z, xkeep, skeep, 1),
            ):
                here = pl.ds(pl.multiple_of((block_z * 2 + core) * depth, 128), depth)
                there = pl.ds(pl.multiple_of((block_z * 2 + 1 - core) * depth, 128), depth)
                mine[slot, rows, :] = (act_v[rows, here].astype(F32) * scale).astype(BF16)
                other[slot, rows, :] = (act_v[rows, there].astype(F32) * scale).astype(BF16)
            return inner

        lax.fori_loop(0, piece // NORM_ROWS, norm_rows, 0)
        pair_own(c).start()
        trade_away(c).start()
        trade_keep(c).start()
        return carry

    lax.fori_loop(0, PIECES, norm_piece, 0)
    for c in range(PIECES):
        trade_away(c).wait_recv()
        pair_sibling(c).start()

    rows = lax.broadcasted_iota(jnp.int32, (seq, seq), 0)
    columns = lax.broadcasted_iota(jnp.int32, (seq, seq), 1)
    doc_wide = jnp.broadcast_to(doc_ref[...].astype(F32), (seq, seq))
    doc_col = jnp.sum(jnp.where(rows == columns, doc_wide, 0.0), axis=1, keepdims=True)
    mask[...] = jnp.where((columns <= rows) & (doc_wide == doc_col), 1.0, 0.0)

    for c in range(PIECES):
        trade_keep(c).wait_recv()
    near, far = pl.ds(0, 2 * seq), pl.ds(2 * seq, 2 * seq)

    def turn(slot, base, count):
        xt[slot, :, base : base + count] = xkeep[slot, base : base + count, :].T

    for slot in (0, 1):
        turn(slot, 0, 2 * seq)
    load_w.wait()
    send_w.wait_recv()

    def project(base, count):
        part = pl.ds(base, count)
        pacc[part, :] = dot(xkeep[0, part, :], wall[0], ((1,), (0,))) + dot(xkeep[1, part, :], wall[1], ((1,), (0,)))

    project(0, 2 * seq)
    give_own = remote(pacc.at[pl.ds(seq, seq)], part_own, p_send.at[0], p_recv.at[0], sibling)
    give_own.start()
    for c in range(PIECES):
        pair_own(c).wait_recv()
    project(2 * seq, seq)
    for c in range(PIECES):
        pair_sibling(c).wait_recv()
    project(3 * seq, seq)
    give_pair = remote(pacc.at[pl.ds(3 * seq, seq)], part_pair, p_send.at[1], p_recv.at[1], sibling)
    give_pair.start()
    give_pair.wait_recv()
    psend[...] = (pacc[2 * seq : 3 * seq, :] + part_pair[...]).astype(BF16)
    give_back = remote(psend, pz, p_send.at[2], p_recv.at[2], pair)
    give_back.start()
    for slot in (0, 1):
        turn(slot, 2 * seq, 2 * seq)
    load_og.wait()
    give_own.wait_recv()
    give_back.wait_recv()
    projected = (pacc[:seq, :] + part_own[...] + pz[...].astype(F32)).astype(BF16)
    grads = attention_grad(projected, mask[...] > 0.5, tab_ref[...], og_v[...])
    for n, grad_part in enumerate(grads):
        g_ref[:seq, n * hd : (n + 1) * hd] = grad_part
    g_pair = remote(g_ref.at[pl.ds(0, seq)], g_ref.at[pl.ds(2 * seq, seq)], g_send.at[0], g_recv.at[0], pair)
    g_sibling = remote(g_ref.at[pl.ds(0, seq)], g_ref.at[pl.ds(seq, seq)], g_send.at[1], g_recv.at[1], sibling)
    g_on = remote(g_ref.at[pl.ds(2 * seq, seq)], g_ref.at[pl.ds(3 * seq, seq)], g_send.at[2], g_recv.at[2], sibling)
    g_pair.start()
    g_sibling.start()
    g_pair.wait_recv()
    g_on.start()
    g_sibling.wait_recv()
    g_on.wait_recv()

    def rows_of(i):
        return pl.ds(pl.multiple_of(i * chunk, 16), chunk)

    def term(slot, rows):
        return dot(xt[slot, rows, :], g_ref[...], ((1,), (0,)))

    def rs_copy(i):
        return remote(tsend.at[rows_of(i)], trecv.at[rows_of(i)], rs_send.at[i], rs_recv.at[i], following)

    def swap_copy(i):
        return remote(upd.at[rows_of(i)], prt.at[rows_of(i)], sw_send.at[i], sw_recv.at[i], partner)

    def out_copies(i):
        return [
            pltpu.make_async_copy(first_o.at[rows_of(i)], first_out.at[rows_of(i)], out_sem.at[0, i]),
            pltpu.make_async_copy(second_o.at[rows_of(i)], second_out.at[rows_of(i)], out_sem.at[1, i]),
        ]

    def mix_copy(i):
        return pltpu.make_async_copy(mix_v.at[rows_of(i)], mixed_hbm.at[rows_of(i)], out_sem.at[2, i])

    def send_terms(i, carry):
        tsend[rows_of(i), :] = term(1, rows_of(i)).astype(BF16)
        rs_copy(i).start()
        return carry

    lax.fori_loop(0, STAGES, send_terms, 0)

    load_first.wait()
    load_second.wait()
    fix_one, fix_two = coef_ref[0], coef_ref[1]

    def update(i, carry):
        rows = rows_of(i)
        grad = term(0, rows)
        rs_copy(i).wait_recv()
        grad = grad + trecv[rows, :].astype(F32)
        weights = wall[0, rows, :].astype(F32)
        first_new = BETA_ONE * first_v[rows, :].astype(F32) + (1.0 - BETA_ONE) * grad
        second_new = BETA_TWO * second_v[rows, :].astype(F32) + (1.0 - BETA_TWO) * grad * grad
        first_hat = first_new / fix_one
        second_hat = second_new / fix_two
        updated = weights - LEARN_RATE * (first_hat / (jnp.sqrt(second_hat) + ADAM_EPS) + DECAY_RATE * weights)
        upd[rows, :] = updated.astype(BF16)
        swap_copy(i).start()
        first_o[rows, :] = first_new.astype(BF16)
        second_o[rows, :] = second_new.astype(BF16)
        for copy in out_copies(i):
            copy.start()
        return carry

    def mix(i, carry):
        rows = rows_of(i)
        swap_copy(i).wait_recv()
        mix_v[rows, :] = ((upd[rows, :].astype(F32) + prt[rows, :].astype(F32)) * 0.5).astype(BF16)
        mix_copy(i).start()
        return carry

    def update_and_mix(i, carry):
        update(i, carry)
        return mix(i - 1, carry)

    update(0, 0)
    lax.fori_loop(1, STAGES, update_and_mix, 0)
    mix(STAGES - 1, 0)

    for copy in (send_w, give_own, give_pair, give_back, g_pair, g_sibling, g_on):
        copy.wait_send()
    for c in range(PIECES):
        for copy in (trade_away(c), trade_keep(c), pair_own(c), pair_sibling(c)):
            copy.wait_send()

    def finish(i, carry):
        rs_copy(i).wait_send()
        swap_copy(i).wait_send()
        for copy in out_copies(i):
            copy.wait()
        mix_copy(i).wait()
        return carry

    lax.fori_loop(0, STAGES, finish, 0)


def per_device(activations, doc_ids, step_index, proj_weights, first_moment, second_moment, out_grad):
    hops = lax.axis_size("fsdp") // 2
    seq, width = activations.shape[1:]
    depth, cols = proj_weights.shape[1:]
    count = (step_index[0] + 1).astype(F32)
    coef = jnp.stack([1.0 - jnp.power(BETA_ONE, count), 1.0 - jnp.power(BETA_TWO, count)])
    tables = jnp.asarray(rotary_tables(seq, cols // 3))
    dma, vmem = pltpu.SemaphoreType.DMA, pltpu.VMEM
    row_vmem = vmem((depth, cols), BF16)
    row_block = jax.ShapeDtypeStruct((depth, cols), BF16)

    def branch(bit):
        return pl.pallas_call(
            functools.partial(kernel, bit, hops),
            out_shape=(row_block, row_block, row_block),
            in_specs=[
                pl.BlockSpec(memory_space=pltpu.SMEM),
                pl.BlockSpec(memory_space=pltpu.VMEM),
                pl.BlockSpec(memory_space=pltpu.VMEM),
            ]
            + [pl.BlockSpec(memory_space=pl.ANY)] * 5,
            out_specs=(pl.BlockSpec(memory_space=pl.ANY),) * 3,
            scratch_shapes=[
                vmem((seq, width), BF16),
                vmem((2, 4 * seq, depth), BF16),
                vmem((2, 2 * seq, depth), BF16),
                vmem((2, seq, depth), BF16),
                vmem((2, seq, depth), BF16),
                vmem((2, depth, 4 * seq), BF16),
                vmem((2, depth, cols), BF16),
                vmem((seq, seq), F32),
                vmem((4 * seq, cols), F32),
                vmem((seq, cols), F32),
                vmem((seq, cols), F32),
                vmem((seq, cols), BF16),
                vmem((seq, cols), BF16),
                vmem((4 * seq, cols), BF16),
                row_vmem,
                row_vmem,
                row_vmem,
                row_vmem,
                vmem((seq, cols // 3), BF16),
                row_vmem,
                row_vmem,
                row_vmem,
                row_vmem,
                row_vmem,
                dma((5,)),
                dma((3, STAGES)),
                dma((2,)),
                dma((4, PIECES)),
                dma((4, PIECES)),
                dma((3,)),
                dma((3,)),
                dma((3,)),
                dma((3,)),
                dma((STAGES,)),
                dma((STAGES,)),
                dma((STAGES,)),
                dma((STAGES,)),
            ],
            compiler_params=pltpu.CompilerParams(
                collective_id=bit, has_side_effects=True, vmem_limit_bytes=40 * 2**20
            ),
        )

    bit_total = lax.axis_size("rep").bit_length() - 1
    outs = lax.switch(
        step_index[0] % bit_total,
        [branch(bit) for bit in range(bit_total)],
        coef, doc_ids, tables, activations[0], proj_weights[0], first_moment[0], second_moment[0], out_grad[0],
    )
    return tuple(out[None] for out in outs)


def solution(mesh):
    rows = P("rep", "fsdp", None)
    return jax.shard_map(
        per_device,
        mesh=mesh,
        in_specs=(rows, P("rep", "fsdp"), P(), rows, rows, rows, rows),
        out_specs=(rows, rows, rows),
        check_vma=False,
    )
```

```python
import functools

import jax
import jax.numpy as jnp
import numpy as np
from jax import lax
from jax.experimental import pallas as pl
from jax.experimental.pallas import tpu as pltpu
from jax.sharding import PartitionSpec as P

BETA_ONE = 0.9
BETA_TWO = 0.95
LEARN_RATE = 0.002
DECAY_RATE = 0.1
ADAM_EPS = 1e-08

MESH = pl.DeviceIdType.MESH
F32 = jnp.float32
BF16 = jnp.bfloat16
PIECES = 2
NORM_ROWS = 32
PART = 256
CHUNK = 64


def rotary_tables(length, head_dim):
    position = np.arange(length, dtype=np.float32)
    inverse = np.float32(10000.0) ** (-(np.arange(head_dim // 2, dtype=np.float32) * np.float32(2.0 / head_dim)))
    angles = (position[:, None] * inverse[None, :]).astype(np.float32)
    cosine, sine = np.cos(angles), np.sin(angles)
    return np.concatenate([cosine, cosine, -sine, sine], axis=1).astype(np.float32)


def dot(a, b, contract, precision=None):
    return lax.dot_general(a, b, ((contract[0], contract[1]), ((), ())), precision=precision, preferred_element_type=F32)


def attention_grad(projected, allowed, tables, out_grad):
    length, width = projected.shape
    hd = width // 3
    high = lax.Precision.HIGHEST
    cosine, sine = tables[:, :hd], tables[:, hd:]

    def rotate(x):
        return x * cosine + pltpu.roll(x, hd // 2, 1) * sine

    def rotate_back(x):
        return x * cosine - pltpu.roll(x, hd // 2, 1) * sine

    query = rotate(projected[:, :hd].astype(F32))
    keys = rotate(projected[:, hd : 2 * hd].astype(F32))
    values = projected[:, 2 * hd :]
    scale = hd ** (-0.5)
    scores = dot(query, keys, ((1,), (1,)), high) * scale
    scores = jnp.where(allowed, scores, -1e30)
    expo = jnp.exp(scores - jnp.max(scores, axis=1, keepdims=True))
    probs = expo / jnp.sum(expo, axis=1, keepdims=True)
    probs_low = probs.astype(BF16)
    grad_values = dot(probs_low, out_grad, ((0,), (0,)))
    grad_probs = dot(out_grad, values, ((1,), (1,)))
    inner = jnp.sum(grad_probs * probs, axis=1, keepdims=True)
    grad_scores = probs * (grad_probs - inner) * scale
    grad_query = rotate_back(dot(grad_scores, keys, ((1,), (0,)), high))
    grad_keys = rotate_back(dot(grad_scores, query, ((0,), (0,)), high))
    return grad_query.astype(BF16), grad_keys.astype(BF16), grad_values.astype(BF16)


def kernel(
    bit, hops,
    coef_ref, doc_ref, tab_ref, act_hbm, w_hbm, first_hbm, second_hbm, og_hbm,
    mixed_hbm, first_out, second_out,
    act_v, keep0, keep1, away0, away1, skeep0, skeep1, saway0, saway1, xt0, xt1, w_own, w0, w1,
    mask, pacc, pacc0, pacc1, rec, rec0, rec1, psend, pz, g_ref,
    tsend, trecv, first_v, second_v, og_v, upd, prt, mix_v, first_o, second_o,
    loc_sem, out_sem, w_send, w_recv, x_send, x_recv, p_send, p_recv, g_send, g_recv, rs_send, rs_recv, sw_send, sw_recv,
):
    rep = lax.axis_index("rep")
    own = lax.axis_index("fsdp")
    z, core = own // 2, own % 2
    step = 1 - 2 * ((z + core) % 2)
    z0, z1, far = (z + step + hops) % hops, (z - step + hops) % hops, (z + 2) % hops
    side0 = (rep, z0 * 2 + core)
    side1 = (rep, z1 * 2 + core)
    sibling = (rep, z * 2 + (1 - core))
    distance = 2**bit
    partner = (rep + (1 - 2 * ((rep // distance) % 2)) * distance, own)
    seq, width = act_v.shape
    depth, cols = w_own.shape
    depth0, depth1 = w0.shape[0], w1.shape[0]
    hd = cols // 3
    chunks0, chunks1 = depth0 // CHUNK, depth1 // CHUNK

    def remote(src, dst, send, recv, device):
        return pltpu.make_async_remote_copy(
            src_ref=src, dst_ref=dst, send_sem=send, recv_sem=recv, device_id=device, device_id_type=MESH
        )

    load_act = pltpu.make_async_copy(act_hbm, act_v, loc_sem.at[0])
    load_w = pltpu.make_async_copy(w_hbm, w_own, loc_sem.at[1])
    load_first = pltpu.make_async_copy(first_hbm, first_v, loc_sem.at[2])
    load_second = pltpu.make_async_copy(second_hbm, second_v, loc_sem.at[3])
    load_og = pltpu.make_async_copy(og_hbm, og_v, loc_sem.at[4])
    for load in (load_act, load_w, load_first, load_second, load_og):
        load.start()

    barrier = pltpu.get_barrier_semaphore()
    for device in (side0, side1, sibling, partner):
        pl.semaphore_signal(barrier, inc=1, device_id=device, device_id_type=MESH)
    pl.semaphore_wait(barrier, 4)

    send_w0 = remote(w_hbm.at[pl.ds(0, depth0)], w0, w_send.at[0], w_recv.at[0], side1)
    send_w1 = remote(w_hbm.at[pl.ds(depth0, depth1)], w1, w_send.at[1], w_recv.at[1], side0)
    send_w0.start()
    send_w1.start()

    load_act.wait()
    piece = seq // PIECES

    def rows_at(base, c):
        return pl.ds(pl.multiple_of(base + c * piece, 16), piece)

    def to_sibling(n, c):
        src, dst = ((saway0, away0), (saway1, away1), (skeep0, keep0), (skeep1, keep1))[n]
        return remote(src.at[:, rows_at(0, c)], dst.at[:, rows_at(seq, c)], x_send.at[n, c], x_recv.at[n, c], sibling)

    def to_pair(part, second, c):
        src, dst, device = ((away0, keep0, side0), (away1, keep1, side1))[part]
        n = 4 + 2 * part + second
        return remote(
            src.at[:, rows_at(second * seq, c)], dst.at[:, rows_at((2 + second) * seq, c)],
            x_send.at[n, c], x_recv.at[n, c], device,
        )

    mine = ((z, keep0, 0, keep1, 0), (z0, away0, 0, keep1, 1), (z1, keep0, 1, away1, 0), (far, away0, 1, away1, 1))
    other = ((z, skeep0, 0, skeep1, 0), (z0, skeep0, 1, saway1, 0), (z1, saway0, 0, skeep1, 1), (far, saway0, 1, saway1, 1))

    def norm_piece(c, carry):
        def norm_rows(i, inner):
            rows = pl.ds(pl.multiple_of(c * piece + i * NORM_ROWS, 16), NORM_ROWS)
            values = act_v[rows, :].astype(F32)
            scale = lax.rsqrt(jnp.sum(values * values, axis=-1, keepdims=True) * (1.0 / width) + 1e-05)
            for places, which in ((mine, core), (other, 1 - core)):
                for chip, ref0, slot0, ref1, slot1 in places:
                    base = (chip * 2 + which) * depth
                    cols0 = pl.ds(pl.multiple_of(base, 128), depth0)
                    cols1 = pl.ds(pl.multiple_of(base + depth0, 128), depth1)
                    ref0[slot0, rows, :] = (act_v[rows, cols0].astype(F32) * scale).astype(BF16)
                    ref1[slot1, rows, :] = (act_v[rows, cols1].astype(F32) * scale).astype(BF16)
            return inner

        lax.fori_loop(0, piece // NORM_ROWS, norm_rows, 0)
        to_pair(0, 0, c).start()
        to_pair(1, 0, c).start()
        for n in range(4):
            to_sibling(n, c).start()
        return carry

    lax.fori_loop(0, PIECES, norm_piece, 0)
    for c in range(PIECES):
        for part in (0, 1):
            to_sibling(part, c).wait_recv()
            to_pair(part, 1, c).start()

    rows = lax.broadcasted_iota(jnp.int32, (seq, seq), 0)
    columns = lax.broadcasted_iota(jnp.int32, (seq, seq), 1)
    doc_wide = jnp.broadcast_to(doc_ref[...].astype(F32), (seq, seq))
    doc_col = jnp.sum(jnp.where(rows == columns, doc_wide, 0.0), axis=1, keepdims=True)
    mask[...] = jnp.where((columns <= rows) & (doc_wide == doc_col), 1.0, 0.0)

    for c in range(PIECES):
        for n in (2, 3):
            to_sibling(n, c).wait_recv()

    def turn(base):
        for keep, xt in ((keep0, xt0), (keep1, xt1)):
            for slot in (0, 1):
                xt[slot, :, base : base + 2 * seq] = keep[slot, base : base + 2 * seq, :].T

    turn(0)
    load_w.wait()
    send_w0.wait_recv()
    send_w1.wait_recv()
    plain = ((1,), (0,))

    def project0(base, count):
        part = pl.ds(base, count)
        return dot(keep0[0, part, :], w_own[:depth0, :], plain) + dot(keep0[1, part, :], w0[...], plain)

    def project1(base, count):
        part = pl.ds(base, count)
        return dot(keep1[0, part, :], w_own[depth0:, :], plain) + dot(keep1[1, part, :], w1[...], plain)

    pacc[...] = project0(0, 2 * seq) + project1(0, 2 * seq)
    low, high = pl.ds(0, seq), pl.ds(seq, seq)
    give = remote(pacc.at[high], rec, p_send.at[0], p_recv.at[0], sibling)
    give.start()
    for c in range(PIECES):
        to_pair(0, 0, c).wait_recv()
    pacc0[low, :] = project0(2 * seq, seq)
    for c in range(PIECES):
        to_pair(1, 0, c).wait_recv()
    pacc1[low, :] = project1(2 * seq, seq)
    for c in range(PIECES):
        to_pair(0, 1, c).wait_recv()
    pacc0[high, :] = project0(3 * seq, seq)
    give0 = remote(pacc0.at[high], rec1, p_send.at[1], p_recv.at[1], sibling)
    give0.start()
    for c in range(PIECES):
        to_pair(1, 1, c).wait_recv()
    pacc1[high, :] = project1(3 * seq, seq)
    give1 = remote(pacc1.at[high], rec0, p_send.at[2], p_recv.at[2], sibling)
    give1.start()
    give0.wait_recv()
    psend[1] = (pacc1[low, :] + rec1[...]).astype(BF16)
    back1 = remote(psend.at[1], pz.at[1], p_send.at[3], p_recv.at[3], side1)
    back1.start()
    give1.wait_recv()
    psend[0] = (pacc0[low, :] + rec0[...]).astype(BF16)
    back0 = remote(psend.at[0], pz.at[0], p_send.at[4], p_recv.at[4], side0)
    back0.start()
    turn(2 * seq)
    load_og.wait()
    give.wait_recv()
    back0.wait_recv()
    back1.wait_recv()
    projected = (pacc[low, :] + rec[...] + pz[0].astype(F32) + pz[1].astype(F32)).astype(BF16)
    grads = attention_grad(projected, mask[...] > 0.5, tab_ref[...], og_v[...])
    for n, grad_part in enumerate(grads):
        g_ref[:seq, n * hd : (n + 1) * hd] = grad_part

    def g_rows(n):
        return g_ref.at[pl.ds(n * seq, seq)]

    g_copies = [
        remote(g_rows(src), g_rows(dst), g_send.at[n], g_recv.at[n], device)
        for n, (src, dst, device) in enumerate(
            ((0, 2, side0), (0, 4, side1), (0, 1, sibling), (2, 5, sibling), (4, 3, sibling))
        )
    ]
    for n in (0, 1, 2):
        g_copies[n].start()
    g_copies[0].wait_recv()
    g_copies[3].start()
    g_copies[1].wait_recv()
    g_copies[4].start()
    for n in (2, 3, 4):
        g_copies[n].wait_recv()

    def part_rows(i):
        return pl.ds(pl.multiple_of(i * CHUNK, 16), CHUNK)

    def rows_of(part, i):
        return pl.ds(pl.multiple_of(part * depth0 + i * CHUNK, 16), CHUNK)

    def term(slot, part, i):
        if part == 0:
            return dot(xt0[slot, part_rows(i), :], g_ref[: 4 * seq, :], plain)
        return dot(xt1[slot, part_rows(i), : 2 * seq], g_ref[: 2 * seq, :], plain) + dot(
            xt1[slot, part_rows(i), 2 * seq :], g_ref[4 * seq :, :], plain
        )

    def rs_copy(part, i):
        rows = rows_of(part, i)
        device = (side1, side0)[part]
        return remote(tsend.at[rows], trecv.at[rows], rs_send.at[part, i], rs_recv.at[part, i], device)

    def swap_copy(part, i):
        rows = rows_of(part, i)
        return remote(upd.at[rows], prt.at[rows], sw_send.at[part, i], sw_recv.at[part, i], partner)

    def out_copies(part, i):
        rows = rows_of(part, i)
        return [
            pltpu.make_async_copy(first_o.at[rows], first_out.at[rows], out_sem.at[0, part, i]),
            pltpu.make_async_copy(second_o.at[rows], second_out.at[rows], out_sem.at[1, part, i]),
        ]

    def mix_copy(part, i):
        rows = rows_of(part, i)
        return pltpu.make_async_copy(mix_v.at[rows], mixed_hbm.at[rows], out_sem.at[2, part, i])

    def send_term(part, i):
        tsend[rows_of(part, i), :] = term(1, part, i).astype(BF16)
        rs_copy(part, i).start()

    def update(part, i):
        rows = rows_of(part, i)
        grad = term(0, part, i)
        rs_copy(part, i).wait_recv()
        grad = grad + trecv[rows, :].astype(F32)
        weights = w_own[rows, :].astype(F32)
        first_new = BETA_ONE * first_v[rows, :].astype(F32) + (1.0 - BETA_ONE) * grad
        second_new = BETA_TWO * second_v[rows, :].astype(F32) + (1.0 - BETA_TWO) * grad * grad
        first_hat = first_new / coef_ref[0]
        second_hat = second_new / coef_ref[1]
        updated = weights - LEARN_RATE * (first_hat / (jnp.sqrt(second_hat) + ADAM_EPS) + DECAY_RATE * weights)
        upd[rows, :] = updated.astype(BF16)
        swap_copy(part, i).start()
        first_o[rows, :] = first_new.astype(BF16)
        second_o[rows, :] = second_new.astype(BF16)
        for copy in out_copies(part, i):
            copy.start()

    def mix(part, i):
        rows = rows_of(part, i)
        swap_copy(part, i).wait_recv()
        mix_v[rows, :] = ((upd[rows, :].astype(F32) + prt[rows, :].astype(F32)) * 0.5).astype(BF16)
        mix_copy(part, i).start()

    def finish(part, i):
        rs_copy(part, i).wait_send()
        swap_copy(part, i).wait_send()
        for copy in out_copies(part, i):
            copy.wait()
        mix_copy(part, i).wait()

    def over_chunks(*calls):
        def both(i, carry):
            for call in calls:
                call(0, i)
                call(1, i)
            return carry

        def rest(i, carry):
            for call in calls:
                call(1, i)
            return carry

        lax.fori_loop(0, chunks0, both, 0)
        lax.fori_loop(chunks0, chunks1, rest, 0)

    over_chunks(send_term)
    load_first.wait()
    load_second.wait()

    update(0, 0)
    update(1, 0)

    def steady(i, carry):
        update(0, i)
        mix(0, i - 1)
        update(1, i)
        mix(1, i - 1)
        return carry

    def steady_rest(i, carry):
        update(1, i)
        mix(1, i - 1)
        return carry

    lax.fori_loop(1, chunks0, steady, 0)
    mix(0, chunks0 - 1)
    lax.fori_loop(chunks0, chunks1, steady_rest, 0)
    mix(1, chunks1 - 1)

    for copy in [send_w0, send_w1, give, give0, give1, back0, back1] + g_copies:
        copy.wait_send()
    for c in range(PIECES):
        for n in range(4):
            to_sibling(n, c).wait_send()
        for part in (0, 1):
            to_pair(part, 0, c).wait_send()
            to_pair(part, 1, c).wait_send()
    over_chunks(finish)


def per_device(activations, doc_ids, step_index, proj_weights, first_moment, second_moment, out_grad):
    hops = lax.axis_size("fsdp") // 2
    seq, width = activations.shape[1:]
    depth, cols = proj_weights.shape[1:]
    count = (step_index[0] + 1).astype(F32)
    coef = jnp.stack([1.0 - jnp.power(BETA_ONE, count), 1.0 - jnp.power(BETA_TWO, count)])
    tables = jnp.asarray(rotary_tables(seq, cols // 3))
    dma, vmem = pltpu.SemaphoreType.DMA, pltpu.VMEM
    rest = depth - PART
    stages = max(PART, rest) // CHUNK
    row_vmem = vmem((depth, cols), BF16)
    row_block = jax.ShapeDtypeStruct((depth, cols), BF16)

    def branch(bit):
        return pl.pallas_call(
            functools.partial(kernel, bit, hops),
            out_shape=(row_block, row_block, row_block),
            in_specs=[
                pl.BlockSpec(memory_space=pltpu.SMEM),
                pl.BlockSpec(memory_space=pltpu.VMEM),
                pl.BlockSpec(memory_space=pltpu.VMEM),
            ]
            + [pl.BlockSpec(memory_space=pl.ANY)] * 5,
            out_specs=(pl.BlockSpec(memory_space=pl.ANY),) * 3,
            scratch_shapes=[
                vmem((seq, width), BF16),
                vmem((2, 4 * seq, PART), BF16),
                vmem((2, 4 * seq, rest), BF16),
                vmem((2, 2 * seq, PART), BF16),
                vmem((2, 2 * seq, rest), BF16),
                vmem((2, seq, PART), BF16),
                vmem((2, seq, rest), BF16),
                vmem((2, seq, PART), BF16),
                vmem((2, seq, rest), BF16),
                vmem((2, PART, 4 * seq), BF16),
                vmem((2, rest, 4 * seq), BF16),
                row_vmem,
                vmem((PART, cols), BF16),
                vmem((rest, cols), BF16),
                vmem((seq, seq), F32),
                vmem((2 * seq, cols), F32),
                vmem((2 * seq, cols), F32),
                vmem((2 * seq, cols), F32),
                vmem((seq, cols), F32),
                vmem((seq, cols), F32),
                vmem((seq, cols), F32),
                vmem((2, seq, cols), BF16),
                vmem((2, seq, cols), BF16),
                vmem((6 * seq, cols), BF16),
                row_vmem,
                row_vmem,
                row_vmem,
                row_vmem,
                vmem((seq, cols // 3), BF16),
                row_vmem,
                row_vmem,
                row_vmem,
                row_vmem,
                row_vmem,
                dma((5,)),
                dma((3, 2, stages)),
                dma((2,)),
                dma((2,)),
                dma((8, PIECES)),
                dma((8, PIECES)),
                dma((5,)),
                dma((5,)),
                dma((5,)),
                dma((5,)),
                dma((2, stages)),
                dma((2, stages)),
                dma((2, stages)),
                dma((2, stages)),
            ],
            compiler_params=pltpu.CompilerParams(
                collective_id=bit, has_side_effects=True, vmem_limit_bytes=40 * 2**20
            ),
        )

    bit_total = lax.axis_size("rep").bit_length() - 1
    outs = lax.switch(
        step_index[0] % bit_total,
        [branch(bit) for bit in range(bit_total)],
        coef, doc_ids, tables, activations[0], proj_weights[0], first_moment[0], second_moment[0], out_grad[0],
    )
    return tuple(out[None] for out in outs)


def solution(mesh):
    rows = P("rep", "fsdp", None)
    return jax.shard_map(
        per_device,
        mesh=mesh,
        in_specs=(rows, P("rep", "fsdp"), P(), rows, rows, rows, rows),
        out_specs=(rows, rows, rows),
        check_vma=False,
    )
```

```python
import functools
import math

import jax
import jax.numpy as jnp
import numpy as np
from jax import lax
from jax.experimental import pallas as pl
from jax.experimental.pallas import tpu as pltpu
from jax.sharding import PartitionSpec as P

BETA_ONE = 0.9
BETA_TWO = 0.95
LEARN_RATE = 0.002
DECAY_RATE = 0.1
ADAM_EPS = 1e-08

MESH = pl.DeviceIdType.MESH
F32 = jnp.float32
BF16 = jnp.bfloat16
PIECES = 2
NORM_ROWS = 32
PART = 256
CHUNK = 64
AHEAD = 3
LAG = 2
MIX_LAG = 2
LOG_ONE = math.log(BETA_ONE)
LOG_TWO = math.log(BETA_TWO)


def rotary_tables(length, head_dim):
    position = np.arange(length, dtype=np.float32)
    inverse = np.float32(10000.0) ** (-(np.arange(head_dim // 2, dtype=np.float32) * np.float32(2.0 / head_dim)))
    angles = (position[:, None] * inverse[None, :]).astype(np.float32)
    cosine, sine = np.cos(angles), np.sin(angles)
    return np.concatenate([cosine, cosine, -sine, sine], axis=1).astype(np.float32)


def dot(a, b, contract, precision=None):
    return lax.dot_general(a, b, ((contract[0], contract[1]), ((), ())), precision=precision, preferred_element_type=F32)


def attention_grad(projected, allowed, tables, out_grad):
    length, width = projected.shape
    hd = width // 3
    high = lax.Precision.HIGHEST
    cosine, sine = tables[:, :hd], tables[:, hd:]

    def rotate(x):
        return x * cosine + pltpu.roll(x, hd // 2, 1) * sine

    def rotate_back(x):
        return x * cosine - pltpu.roll(x, hd // 2, 1) * sine

    query = rotate(projected[:, :hd].astype(F32))
    keys = rotate(projected[:, hd : 2 * hd].astype(F32))
    values = projected[:, 2 * hd :]
    scale = hd ** (-0.5)
    scores = dot(query, keys, ((1,), (1,)), high) * scale
    scores = jnp.where(allowed, scores, -1e30)
    expo = jnp.exp(scores - jnp.max(scores, axis=1, keepdims=True))
    probs = expo / jnp.sum(expo, axis=1, keepdims=True)
    probs_low = probs.astype(BF16)
    grad_values = dot(probs_low, out_grad, ((0,), (0,)))
    grad_probs = dot(out_grad, values, ((1,), (1,)))
    inner = jnp.sum(grad_probs * probs, axis=1, keepdims=True)
    grad_scores = probs * (grad_probs - inner) * scale
    grad_query = rotate_back(dot(grad_scores, keys, ((1,), (0,)), high))
    grad_keys = rotate_back(dot(grad_scores, query, ((0,), (0,)), high))
    return grad_query.astype(BF16), grad_keys.astype(BF16), grad_values.astype(BF16)


def kernel(
    bit, hops,
    step_ref, doc_ref, tab_ref, act_hbm, w_hbm, first_hbm, second_hbm, og_hbm,
    mixed_out, first_out, second_out,
    act_v, keep0, keep1, away0, away1, skeep0, skeep1, saway0, saway1, xt0, xt1, w_own, w0, w1,
    mask, pacc, pacc0, pacc1, rec, rec0, rec1, psend, pz, g_ref,
    tsend, trecv, first_v, second_v, og_v, t_own, upd, prt,
    loc_sem, w_send, w_recv, x_send, x_recv, p_send, p_recv, g_send, g_recv, rs_send, rs_recv, sw_send, sw_recv,
):
    rep = lax.axis_index("rep")
    own = lax.axis_index("fsdp")
    z, core = own // 2, own % 2
    step = 1 - 2 * ((z + core) % 2)
    z0, z1, far = (z + step + hops) % hops, (z - step + hops) % hops, (z + 2) % hops
    side0 = (rep, z0 * 2 + core)
    side1 = (rep, z1 * 2 + core)
    sibling = (rep, z * 2 + (1 - core))
    distance = 2**bit
    partner = (rep + (1 - 2 * ((rep // distance) % 2)) * distance, own)
    seq, width = act_v.shape
    depth, cols = w_own.shape
    depth0, depth1 = w0.shape[0], w1.shape[0]
    hd = cols // 3
    chunks0, chunks1 = depth0 // CHUNK, depth1 // CHUNK

    def remote(src, dst, send, recv, device):
        return pltpu.make_async_remote_copy(
            src_ref=src, dst_ref=dst, send_sem=send, recv_sem=recv, device_id=device, device_id_type=MESH
        )

    load_act = pltpu.make_async_copy(act_hbm, act_v, loc_sem.at[0])
    load_w = pltpu.make_async_copy(w_hbm, w_own, loc_sem.at[1])
    load_first = pltpu.make_async_copy(first_hbm, first_v, loc_sem.at[2])
    load_second = pltpu.make_async_copy(second_hbm, second_v, loc_sem.at[3])
    load_og = pltpu.make_async_copy(og_hbm, og_v, loc_sem.at[4])
    for load in (load_act, load_w, load_first, load_second, load_og):
        load.start()

    barrier = pltpu.get_barrier_semaphore()
    for device in (side0, side1, sibling, partner):
        pl.semaphore_signal(barrier, inc=1, device_id=device, device_id_type=MESH)
    pl.semaphore_wait(barrier, 4)

    send_w0 = remote(w_hbm.at[pl.ds(0, depth0)], w0, w_send.at[0], w_recv.at[0], side1)
    send_w1 = remote(w_hbm.at[pl.ds(depth0, depth1)], w1, w_send.at[1], w_recv.at[1], side0)
    send_w0.start()
    send_w1.start()

    load_act.wait()
    piece = seq // PIECES

    def rows_at(base, c):
        return pl.ds(pl.multiple_of(base + c * piece, 16), piece)

    def to_sibling(n, c):
        src, dst = ((saway0, away0), (saway1, away1), (skeep0, keep0), (skeep1, keep1))[n]
        return remote(src.at[:, rows_at(0, c)], dst.at[:, rows_at(seq, c)], x_send.at[n, c], x_recv.at[n, c], sibling)

    def to_pair(part, second, c):
        src, dst, device = ((away0, keep0, side0), (away1, keep1, side1))[part]
        n = 4 + 2 * part + second
        return remote(
            src.at[:, rows_at(second * seq, c)], dst.at[:, rows_at((2 + second) * seq, c)],
            x_send.at[n, c], x_recv.at[n, c], device,
        )

    mine = ((z, keep0, 0, keep1, 0), (z0, away0, 0, keep1, 1), (z1, keep0, 1, away1, 0), (far, away0, 1, away1, 1))
    other = ((z, skeep0, 0, skeep1, 0), (z0, skeep0, 1, saway1, 0), (z1, saway0, 0, skeep1, 1), (far, saway0, 1, saway1, 1))

    def norm_piece(c, carry):
        def norm_rows(i, inner):
            rows = pl.ds(pl.multiple_of(c * piece + i * NORM_ROWS, 16), NORM_ROWS)
            values = act_v[rows, :].astype(F32)
            scale = lax.rsqrt(jnp.sum(values * values, axis=-1, keepdims=True) * (1.0 / width) + 1e-05)
            for places, which in ((mine, core), (other, 1 - core)):
                for chip, ref0, slot0, ref1, slot1 in places:
                    base = (chip * 2 + which) * depth
                    cols0 = pl.ds(pl.multiple_of(base, 128), depth0)
                    cols1 = pl.ds(pl.multiple_of(base + depth0, 128), depth1)
                    ref0[slot0, rows, :] = (act_v[rows, cols0].astype(F32) * scale).astype(BF16)
                    ref1[slot1, rows, :] = (act_v[rows, cols1].astype(F32) * scale).astype(BF16)
            return inner

        lax.fori_loop(0, piece // NORM_ROWS, norm_rows, 0)
        to_pair(0, 0, c).start()
        to_pair(1, 0, c).start()
        for n in range(4):
            to_sibling(n, c).start()
        return carry

    lax.fori_loop(0, PIECES, norm_piece, 0)
    for c in range(PIECES):
        for part in (0, 1):
            to_sibling(part, c).wait_recv()
            to_pair(part, 1, c).start()

    rows = lax.broadcasted_iota(jnp.int32, (seq, seq), 0)
    columns = lax.broadcasted_iota(jnp.int32, (seq, seq), 1)
    doc_wide = jnp.broadcast_to(doc_ref[...].astype(F32), (seq, seq))
    doc_col = jnp.sum(jnp.where(rows == columns, doc_wide, 0.0), axis=1, keepdims=True)
    mask[...] = jnp.where((columns <= rows) & (doc_wide == doc_col), 1.0, 0.0)

    for c in range(PIECES):
        for n in (2, 3):
            to_sibling(n, c).wait_recv()

    def turn(base):
        for keep, xt in ((keep0, xt0), (keep1, xt1)):
            for slot in (0, 1):
                xt[slot, :, base : base + 2 * seq] = keep[slot, base : base + 2 * seq, :].T

    turn(0)
    load_w.wait()
    send_w0.wait_recv()
    send_w1.wait_recv()
    plain = ((1,), (0,))

    def project0(base, count):
        part = pl.ds(base, count)
        return dot(keep0[0, part, :], w_own[:depth0, :], plain) + dot(keep0[1, part, :], w0[...], plain)

    def project1(base, count):
        part = pl.ds(base, count)
        return dot(keep1[0, part, :], w_own[depth0:, :], plain) + dot(keep1[1, part, :], w1[...], plain)

    pacc[...] = project0(0, 2 * seq) + project1(0, 2 * seq)
    low, high = pl.ds(0, seq), pl.ds(seq, seq)
    give = remote(pacc.at[high], rec, p_send.at[0], p_recv.at[0], sibling)
    give.start()
    for c in range(PIECES):
        to_pair(0, 0, c).wait_recv()
    pacc0[low, :] = project0(2 * seq, seq)
    for c in range(PIECES):
        to_pair(1, 0, c).wait_recv()
    pacc1[low, :] = project1(2 * seq, seq)
    for c in range(PIECES):
        to_pair(0, 1, c).wait_recv()
    pacc0[high, :] = project0(3 * seq, seq)
    give0 = remote(pacc0.at[high], rec1, p_send.at[1], p_recv.at[1], sibling)
    give0.start()
    for c in range(PIECES):
        to_pair(1, 1, c).wait_recv()
    pacc1[high, :] = project1(3 * seq, seq)
    give1 = remote(pacc1.at[high], rec0, p_send.at[2], p_recv.at[2], sibling)
    give1.start()
    give0.wait_recv()
    psend[1] = (pacc1[low, :] + rec1[...]).astype(BF16)
    back1 = remote(psend.at[1], pz.at[1], p_send.at[3], p_recv.at[3], side1)
    back1.start()
    give1.wait_recv()
    psend[0] = (pacc0[low, :] + rec0[...]).astype(BF16)
    back0 = remote(psend.at[0], pz.at[0], p_send.at[4], p_recv.at[4], side0)
    back0.start()
    turn(2 * seq)
    load_og.wait()
    give.wait_recv()
    back0.wait_recv()
    back1.wait_recv()
    projected = (pacc[low, :] + rec[...] + pz[0].astype(F32) + pz[1].astype(F32)).astype(BF16)
    grads = attention_grad(projected, mask[...] > 0.5, tab_ref[...], og_v[...])
    for n, grad_part in enumerate(grads):
        g_ref[:seq, n * hd : (n + 1) * hd] = grad_part

    def g_rows(n):
        return g_ref.at[pl.ds(n * seq, seq)]

    g_copies = [
        remote(g_rows(src), g_rows(dst), g_send.at[n], g_recv.at[n], device)
        for n, (src, dst, device) in enumerate(
            ((0, 2, side0), (0, 4, side1), (0, 1, sibling), (2, 5, sibling), (4, 3, sibling))
        )
    ]
    for n in (0, 1, 2):
        g_copies[n].start()
    g_copies[0].wait_recv()
    g_copies[3].start()
    g_copies[1].wait_recv()
    g_copies[4].start()
    for n in (2, 3, 4):
        g_copies[n].wait_recv()

    def rows_of(part, i):
        return pl.ds(pl.multiple_of(part * depth0 + i * CHUNK, 16), CHUNK)

    def term(slot, part):
        if part == 0:
            return dot(xt0[slot], g_ref[: 4 * seq, :], plain)
        return dot(xt1[slot, :, : 2 * seq], g_ref[: 2 * seq, :], plain) + dot(
            xt1[slot, :, 2 * seq :], g_ref[4 * seq :, :], plain
        )

    def rs_copy(part, i):
        rows = rows_of(part, i)
        device = (side1, side0)[part]
        return remote(tsend.at[rows], trecv.at[rows], rs_send.at[part, i], rs_recv.at[part, i], device)

    def swap_copy(part, i):
        rows = rows_of(part, i)
        return remote(upd.at[rows], prt.at[rows], sw_send.at[part, i], sw_recv.at[part, i], partner)

    all_rows = (pl.ds(0, depth0), pl.ds(depth0, depth1))
    chunks = (chunks0, chunks1)
    for part in (0, 1):
        tsend[all_rows[part], :] = term(1, part).astype(BF16)
        for i in range(AHEAD):
            rs_copy(part, i).start()
    for part in (0, 1):
        t_own[all_rows[part], :] = term(0, part)
    load_first.wait()
    load_second.wait()
    count = jnp.full((1, cols), step_ref[0] + 1, jnp.int32).astype(F32)
    fix_one = 1.0 - jnp.exp(count * LOG_ONE)
    fix_two = 1.0 - jnp.exp(count * LOG_TWO)

    def update(part, i):
        rows = rows_of(part, i)
        rs_copy(part, i).wait_recv()
        grad = t_own[rows, :] + trecv[rows, :].astype(F32)
        weights = w_own[rows, :].astype(F32)
        first_new = BETA_ONE * first_v[rows, :].astype(F32) + (1.0 - BETA_ONE) * grad
        second_new = BETA_TWO * second_v[rows, :].astype(F32) + (1.0 - BETA_TWO) * grad * grad
        first_hat = first_new / fix_one
        second_hat = second_new / fix_two
        updated = weights - LEARN_RATE * (first_hat / (jnp.sqrt(second_hat) + ADAM_EPS) + DECAY_RATE * weights)
        upd[rows, :] = updated.astype(BF16)
        swap_copy(part, i).start()
        first_out[rows, :] = first_new.astype(BF16)
        second_out[rows, :] = second_new.astype(BF16)

    def mix(part, i):
        rows = rows_of(part, i)
        swap_copy(part, i).wait_recv()
        mixed_out[rows, :] = ((upd[rows, :].astype(F32) + prt[rows, :].astype(F32)) * 0.5).astype(BF16)

    def stage(i, carry):
        for part in (0, 1):

            @pl.when(i < chunks[part] - AHEAD)
            def _():
                rs_copy(part, i).wait_send()
                rs_copy(part, i + AHEAD).start()

        for part in (0, 1):

            @pl.when((i >= LAG) & (i < chunks[part] + LAG))
            def _():
                update(part, i - LAG)

        for part in (0, 1):

            @pl.when((i >= LAG + MIX_LAG) & (i < chunks[part] + LAG + MIX_LAG))
            def _():
                mix(part, i - LAG - MIX_LAG)

        return carry

    lax.fori_loop(0, chunks1 + LAG + MIX_LAG, stage, 0)

    for copy in [send_w0, send_w1, give, give0, give1, back0, back1] + g_copies:
        copy.wait_send()
    for c in range(PIECES):
        for n in range(4):
            to_sibling(n, c).wait_send()
        for part in (0, 1):
            to_pair(part, 0, c).wait_send()
            to_pair(part, 1, c).wait_send()
    for part in (0, 1):
        for i in range(chunks[part] - AHEAD, chunks[part]):
            rs_copy(part, i).wait_send()
        for i in range(chunks[part]):
            swap_copy(part, i).wait_send()


def per_device(activations, doc_ids, step_index, proj_weights, first_moment, second_moment, out_grad):
    hops = lax.axis_size("fsdp") // 2
    seq, width = activations.shape[1:]
    depth, cols = proj_weights.shape[1:]
    tables = jnp.asarray(rotary_tables(seq, cols // 3))
    dma, vmem = pltpu.SemaphoreType.DMA, pltpu.VMEM
    rest = depth - PART
    stages = max(PART, rest) // CHUNK
    row_vmem = vmem((depth, cols), BF16)
    row_block = jax.ShapeDtypeStruct((depth, cols), BF16)

    def branch(bit):
        return pl.pallas_call(
            functools.partial(kernel, bit, hops),
            out_shape=(row_block, row_block, row_block),
            in_specs=[
                pl.BlockSpec(memory_space=pltpu.SMEM),
                pl.BlockSpec(memory_space=pltpu.VMEM),
                pl.BlockSpec(memory_space=pltpu.VMEM),
            ]
            + [pl.BlockSpec(memory_space=pl.ANY)] * 5,
            out_specs=(pl.BlockSpec(memory_space=pltpu.VMEM),) * 3,
            scratch_shapes=[
                vmem((seq, width), BF16),
                vmem((2, 4 * seq, PART), BF16),
                vmem((2, 4 * seq, rest), BF16),
                vmem((2, 2 * seq, PART), BF16),
                vmem((2, 2 * seq, rest), BF16),
                vmem((2, seq, PART), BF16),
                vmem((2, seq, rest), BF16),
                vmem((2, seq, PART), BF16),
                vmem((2, seq, rest), BF16),
                vmem((2, PART, 4 * seq), BF16),
                vmem((2, rest, 4 * seq), BF16),
                row_vmem,
                vmem((PART, cols), BF16),
                vmem((rest, cols), BF16),
                vmem((seq, seq), F32),
                vmem((2 * seq, cols), F32),
                vmem((2 * seq, cols), F32),
                vmem((2 * seq, cols), F32),
                vmem((seq, cols), F32),
                vmem((seq, cols), F32),
                vmem((seq, cols), F32),
                vmem((2, seq, cols), BF16),
                vmem((2, seq, cols), BF16),
                vmem((6 * seq, cols), BF16),
                row_vmem,
                row_vmem,
                row_vmem,
                row_vmem,
                vmem((seq, cols // 3), BF16),
                vmem((depth, cols), F32),
                row_vmem,
                row_vmem,
                dma((5,)),
                dma((2,)),
                dma((2,)),
                dma((8, PIECES)),
                dma((8, PIECES)),
                dma((5,)),
                dma((5,)),
                dma((5,)),
                dma((5,)),
                dma((2, stages)),
                dma((2, stages)),
                dma((2, stages)),
                dma((2, stages)),
            ],
            compiler_params=pltpu.CompilerParams(
                collective_id=bit, has_side_effects=True, vmem_limit_bytes=40 * 2**20
            ),
        )

    bit_total = lax.axis_size("rep").bit_length() - 1
    outs = lax.switch(
        lax.rem(step_index[0], bit_total),
        [branch(bit) for bit in range(bit_total)],
        step_index, doc_ids, tables, activations[0], proj_weights[0], first_moment[0], second_moment[0], out_grad[0],
    )
    return tuple(out[None] for out in outs)


def solution(mesh):
    rows = P("rep", "fsdp", None)
    return jax.shard_map(
        per_device,
        mesh=mesh,
        in_specs=(rows, P("rep", "fsdp"), P(), rows, rows, rows, rows),
        out_specs=(rows, rows, rows),
        check_vma=False,
    )
```

```python
import functools
import math

import jax
import jax.numpy as jnp
import numpy as np
from jax import lax
from jax.experimental import pallas as pl
from jax.experimental.pallas import tpu as pltpu
from jax.sharding import PartitionSpec as P

BETA_ONE = 0.9
BETA_TWO = 0.95
LEARN_RATE = 0.002
DECAY_RATE = 0.1
ADAM_EPS = 1e-08

MESH = pl.DeviceIdType.MESH
F32 = jnp.float32
BF16 = jnp.bfloat16
PIECES = 2
NORM_ROWS = 32
CHUNK = 64
AHEAD = 3
LAG = 2
MIX_LAG = 2
LOG_ONE = math.log(BETA_ONE)
LOG_TWO = math.log(BETA_TWO)


def rotary_tables(length, head_dim):
    position = np.arange(length, dtype=np.float32)
    inverse = np.float32(10000.0) ** (-(np.arange(head_dim // 2, dtype=np.float32) * np.float32(2.0 / head_dim)))
    angles = (position[:, None] * inverse[None, :]).astype(np.float32)
    cosine, sine = np.cos(angles), np.sin(angles)
    return np.concatenate([cosine, cosine, -sine, sine], axis=1).astype(np.float32)


def dot(a, b, contract, precision=None):
    return lax.dot_general(a, b, ((contract[0], contract[1]), ((), ())), precision=precision, preferred_element_type=F32)


def attention_grad(projected, allowed, tables, out_grad):
    length, width = projected.shape
    hd = width // 3
    high = lax.Precision.HIGHEST
    cosine, sine = tables[:, :hd], tables[:, hd:]

    def rotate(x):
        return x * cosine + pltpu.roll(x, hd // 2, 1) * sine

    def rotate_back(x):
        return x * cosine - pltpu.roll(x, hd // 2, 1) * sine

    query = rotate(projected[:, :hd].astype(F32))
    keys = rotate(projected[:, hd : 2 * hd].astype(F32))
    values = projected[:, 2 * hd :]
    scale = hd ** (-0.5)
    scores = dot(query, keys, ((1,), (1,)), high) * scale
    scores = jnp.where(allowed, scores, -1e30)
    expo = jnp.exp(scores - jnp.max(scores, axis=1, keepdims=True))
    probs = expo / jnp.sum(expo, axis=1, keepdims=True)
    probs_low = probs.astype(BF16)
    grad_values = dot(probs_low, out_grad, ((0,), (0,)))
    grad_probs = dot(out_grad, values, ((1,), (1,)))
    inner = jnp.sum(grad_probs * probs, axis=1, keepdims=True)
    grad_scores = probs * (grad_probs - inner) * scale
    grad_query = rotate_back(dot(grad_scores, keys, ((1,), (0,)), high))
    grad_keys = rotate_back(dot(grad_scores, query, ((0,), (0,)), high))
    return grad_query.astype(BF16), grad_keys.astype(BF16), grad_values.astype(BF16)


def kernel(
    bit, hops,
    step_ref, doc_ref, tab_ref, act_hbm, w_hbm, first_hbm, second_hbm, og_hbm,
    out_ref,
    act_v, keep, to_pair, to_cross, to_sib, xt, wall, mask, pacc, rec, psend, pz, g_ref,
    tsend, trecv, first_v, second_v, og_v, t_own, upd, prt,
    loc_sem, w_sem, x_send, x_recv, p_send, p_recv, g_send, g_recv, rs_send, rs_recv, sw_send, sw_recv,
):
    rep = lax.axis_index("rep")
    own = lax.axis_index("fsdp")
    z, core = own // 2, own % 2
    step = 1 - 2 * ((z + core) % 2)
    z_pair, z_next, z_far = (z + step + hops) % hops, (z - step + hops) % hops, (z + 2) % hops
    pair = (rep, z_pair * 2 + core)
    pair_cross = (rep, z_pair * 2 + 1 - core)
    following = (rep, z_next * 2 + core)
    next_cross = (rep, z_next * 2 + 1 - core)
    sibling = (rep, z * 2 + (1 - core))
    distance = 2**bit
    partner = (rep + (1 - 2 * ((rep // distance) % 2)) * distance, own)
    seq, width = act_v.shape
    depth, cols = wall.shape[1:]
    hd = cols // 3
    chunks = depth // CHUNK

    def remote(src, dst, send, recv, device):
        return pltpu.make_async_remote_copy(
            src_ref=src, dst_ref=dst, send_sem=send, recv_sem=recv, device_id=device, device_id_type=MESH
        )

    load_act = pltpu.make_async_copy(act_hbm, act_v, loc_sem.at[0])
    load_w = pltpu.make_async_copy(w_hbm, wall.at[0], loc_sem.at[1])
    load_first = pltpu.make_async_copy(first_hbm, first_v, loc_sem.at[2])
    load_second = pltpu.make_async_copy(second_hbm, second_v, loc_sem.at[3])
    load_og = pltpu.make_async_copy(og_hbm, og_v, loc_sem.at[4])
    for load in (load_act, load_w, load_first, load_second, load_og):
        load.start()

    barrier = pltpu.get_barrier_semaphore()
    greeted = (pair, pair_cross, following, next_cross, sibling, partner)
    for device in greeted:
        pl.semaphore_signal(barrier, inc=1, device_id=device, device_id_type=MESH)
    pl.semaphore_wait(barrier, len(greeted))

    send_w = remote(w_hbm, wall.at[1], w_sem.at[0], w_sem.at[1], following)
    send_w.start()

    load_act.wait()
    piece = seq // PIECES

    def rows_at(base, c):
        return pl.ds(pl.multiple_of(base + c * piece, 16), piece)

    def trade(n, c):
        src, base, device = ((to_pair, 2 * seq, pair), (to_cross, 3 * seq, next_cross), (to_sib, seq, sibling))[n]
        return remote(src.at[:, rows_at(0, c)], keep.at[:, rows_at(base, c)], x_send.at[n, c], x_recv.at[n, c], device)

    places = (
        (z_pair, core, to_pair, 0), (z_far, core, to_pair, 1),
        (z_next, 1 - core, to_cross, 0), (z_far, 1 - core, to_cross, 1),
        (z, 1 - core, to_sib, 0), (z_pair, 1 - core, to_sib, 1),
        (z, core, keep, 0), (z_next, core, keep, 1),
    )

    def norm_piece(c, carry):
        def norm_rows(i, inner):
            rows = pl.ds(pl.multiple_of(c * piece + i * NORM_ROWS, 16), NORM_ROWS)
            values = act_v[rows, :].astype(F32)
            scale = lax.rsqrt(jnp.sum(values * values, axis=-1, keepdims=True) * (1.0 / width) + 1e-05)
            for chip, which, ref, slot in places:
                block = pl.ds(pl.multiple_of((chip * 2 + which) * depth, 128), depth)
                ref[slot, rows, :] = (act_v[rows, block].astype(F32) * scale).astype(BF16)
            return inner

        lax.fori_loop(0, piece // NORM_ROWS, norm_rows, 0)
        for n in range(3):
            trade(n, c).start()
        return carry

    lax.fori_loop(0, PIECES, norm_piece, 0)

    rows = lax.broadcasted_iota(jnp.int32, (seq, seq), 0)
    columns = lax.broadcasted_iota(jnp.int32, (seq, seq), 1)
    doc_wide = jnp.broadcast_to(doc_ref[...].astype(F32), (seq, seq))
    doc_col = jnp.sum(jnp.where(rows == columns, doc_wide, 0.0), axis=1, keepdims=True)
    mask[...] = jnp.where((columns <= rows) & (doc_wide == doc_col), 1.0, 0.0)

    for c in range(PIECES):
        trade(2, c).wait_recv()

    def turn(base):
        for slot in (0, 1):
            xt[slot, :, base : base + 2 * seq] = keep[slot, base : base + 2 * seq, :].T

    turn(0)
    load_w.wait()
    send_w.wait_recv()
    plain = ((1,), (0,))

    def project(base, count):
        part = pl.ds(base, count)
        return dot(keep[0, part, :], wall[0], plain) + dot(keep[1, part, :], wall[1], plain)

    pacc[...] = project(0, 2 * seq)
    give = remote(pacc.at[pl.ds(seq, seq)], rec, p_send.at[0], p_recv.at[0], sibling)
    give.start()
    backs = [
        remote(psend.at[n], pz.at[n], p_send.at[1 + n], p_recv.at[1 + n], device)
        for n, device in enumerate((pair, pair_cross))
    ]
    for n in (0, 1):
        for c in range(PIECES):
            trade(n, c).wait_recv()
        psend[n] = project((2 + n) * seq, seq).astype(BF16)
        backs[n].start()
    turn(2 * seq)
    load_og.wait()
    give.wait_recv()
    for copy in backs:
        copy.wait_recv()
    projected = (pacc[:seq, :] + rec[...] + pz[0].astype(F32) + pz[1].astype(F32)).astype(BF16)
    grads = attention_grad(projected, mask[...] > 0.5, tab_ref[...], og_v[...])
    for n, grad_part in enumerate(grads):
        g_ref[:seq, n * hd : (n + 1) * hd] = grad_part

    g_copies = [
        remote(g_ref.at[pl.ds(0, seq)], g_ref.at[pl.ds(base * seq, seq)], g_send.at[n], g_recv.at[n], device)
        for n, (base, device) in enumerate(((2, pair), (3, next_cross), (1, sibling)))
    ]
    for copy in g_copies:
        copy.start()
    for copy in g_copies:
        copy.wait_recv()

    def rows_of(i):
        return pl.ds(pl.multiple_of(i * CHUNK, 16), CHUNK)

    def rs_copy(i):
        return remote(tsend.at[rows_of(i)], trecv.at[rows_of(i)], rs_send.at[i], rs_recv.at[i], following)

    def swap_copy(i):
        return remote(upd.at[rows_of(i)], prt.at[rows_of(i)], sw_send.at[i], sw_recv.at[i], partner)

    half = depth // 2
    for n in (0, 1):
        part = pl.ds(n * half, half)
        tsend[part, :] = dot(xt[1, part, :], g_ref[...], plain).astype(BF16)
        if n == 0:
            for i in range(AHEAD):
                rs_copy(i).start()
    t_own[...] = dot(xt[0], g_ref[...], plain)
    load_first.wait()
    load_second.wait()
    count = jnp.full((1, cols), step_ref[0] + 1, jnp.int32).astype(F32)
    fix_one = 1.0 - jnp.exp(count * LOG_ONE)
    fix_two = 1.0 - jnp.exp(count * LOG_TWO)

    def update(i):
        rows = rows_of(i)
        rs_copy(i).wait_recv()
        grad = t_own[rows, :] + trecv[rows, :].astype(F32)
        weights = wall[0, rows, :].astype(F32)
        first_new = BETA_ONE * first_v[rows, :].astype(F32) + (1.0 - BETA_ONE) * grad
        second_new = BETA_TWO * second_v[rows, :].astype(F32) + (1.0 - BETA_TWO) * grad * grad
        first_hat = first_new / fix_one
        second_hat = second_new / fix_two
        updated = weights - LEARN_RATE * (first_hat / (jnp.sqrt(second_hat) + ADAM_EPS) + DECAY_RATE * weights)
        upd[rows, :] = updated.astype(BF16)
        swap_copy(i).start()
        out_ref[1, rows, :] = first_new.astype(BF16)
        out_ref[2, rows, :] = second_new.astype(BF16)

    def mix(i):
        rows = rows_of(i)
        swap_copy(i).wait_recv()
        out_ref[0, rows, :] = ((upd[rows, :].astype(F32) + prt[rows, :].astype(F32)) * 0.5).astype(BF16)

    def stage(i, carry):
        @pl.when(i < chunks - AHEAD)
        def _():
            rs_copy(i).wait_send()
            rs_copy(i + AHEAD).start()

        @pl.when((i >= LAG) & (i < chunks + LAG))
        def _():
            update(i - LAG)

        @pl.when(i >= LAG + MIX_LAG)
        def _():
            mix(i - LAG - MIX_LAG)

        return carry

    lax.fori_loop(0, chunks + LAG + MIX_LAG, stage, 0)

    for copy in [send_w, give] + backs + g_copies:
        copy.wait_send()
    for c in range(PIECES):
        for n in range(3):
            trade(n, c).wait_send()
    for i in range(chunks - AHEAD, chunks):
        rs_copy(i).wait_send()
    for i in range(chunks):
        swap_copy(i).wait_send()


def per_device(activations, doc_ids, step_index, proj_weights, first_moment, second_moment, out_grad):
    hops = lax.axis_size("fsdp") // 2
    seq, width = activations.shape[1:]
    depth, cols = proj_weights.shape[1:]
    tables = jnp.asarray(rotary_tables(seq, cols // 3))
    dma, vmem = pltpu.SemaphoreType.DMA, pltpu.VMEM
    stages = depth // CHUNK
    row_vmem = vmem((depth, cols), BF16)

    def branch(bit):
        return pl.pallas_call(
            functools.partial(kernel, bit, hops),
            out_shape=jax.ShapeDtypeStruct((3, depth, cols), BF16),
            in_specs=[
                pl.BlockSpec(memory_space=pltpu.SMEM),
                pl.BlockSpec(memory_space=pltpu.VMEM),
                pl.BlockSpec(memory_space=pltpu.VMEM),
            ]
            + [pl.BlockSpec(memory_space=pl.ANY)] * 5,
            out_specs=pl.BlockSpec(memory_space=pltpu.VMEM),
            scratch_shapes=[
                vmem((seq, width), BF16),
                vmem((2, 4 * seq, depth), BF16),
                vmem((2, seq, depth), BF16),
                vmem((2, seq, depth), BF16),
                vmem((2, seq, depth), BF16),
                vmem((2, depth, 4 * seq), BF16),
                vmem((2, depth, cols), BF16),
                vmem((seq, seq), F32),
                vmem((2 * seq, cols), F32),
                vmem((seq, cols), F32),
                vmem((2, seq, cols), BF16),
                vmem((2, seq, cols), BF16),
                vmem((4 * seq, cols), BF16),
                row_vmem,
                row_vmem,
                row_vmem,
                row_vmem,
                vmem((seq, cols // 3), BF16),
                vmem((depth, cols), F32),
                row_vmem,
                row_vmem,
                dma((5,)),
                dma((2,)),
                dma((3, PIECES)),
                dma((3, PIECES)),
                dma((3,)),
                dma((3,)),
                dma((3,)),
                dma((3,)),
                dma((stages,)),
                dma((stages,)),
                dma((stages,)),
                dma((stages,)),
            ],
            compiler_params=pltpu.CompilerParams(
                collective_id=bit, has_side_effects=True, vmem_limit_bytes=40 * 2**20
            ),
        )

    bit_total = lax.axis_size("rep").bit_length() - 1
    outs = lax.switch(
        lax.rem(step_index[0], bit_total),
        [branch(bit) for bit in range(bit_total)],
        step_index, doc_ids, tables, activations[0], proj_weights[0], first_moment[0], second_moment[0], out_grad[0],
    )
    return tuple(outs[n : n + 1] for n in range(3))


def solution(mesh):
    rows = P("rep", "fsdp", None)
    return jax.shard_map(
        per_device,
        mesh=mesh,
        in_specs=(rows, P("rep", "fsdp"), P(), rows, rows, rows, rows),
        out_specs=(rows, rows, rows),
        check_vma=False,
    )
```

```python
import functools
import math

import jax
import jax.numpy as jnp
import numpy as np
from jax import lax
from jax.experimental import pallas as pl
from jax.experimental.pallas import tpu as pltpu
from jax.sharding import PartitionSpec as P

BETA_ONE = 0.9
BETA_TWO = 0.95
LEARN_RATE = 0.002
DECAY_RATE = 0.1
ADAM_EPS = 1e-08

MESH = pl.DeviceIdType.MESH
F32 = jnp.float32
BF16 = jnp.bfloat16
PIECES = 2
NORM_ROWS = 32
CHUNK = 64
AHEAD = 3
LAG = 2
MIX_LAG = 2
LOG_ONE = math.log(BETA_ONE)
LOG_TWO = math.log(BETA_TWO)


def rotary_tables(length, head_dim):
    position = np.arange(length, dtype=np.float32)
    inverse = np.float32(10000.0) ** (-(np.arange(head_dim // 2, dtype=np.float32) * np.float32(2.0 / head_dim)))
    angles = (position[:, None] * inverse[None, :]).astype(np.float32)
    cosine, sine = np.cos(angles), np.sin(angles)
    return np.concatenate([cosine, cosine, -sine, sine], axis=1).astype(np.float32)


def dot(a, b, contract, precision=None):
    return lax.dot_general(a, b, ((contract[0], contract[1]), ((), ())), precision=precision, preferred_element_type=F32)


def attention_grad(projected, allowed, tables, out_grad):
    length, width = projected.shape
    hd = width // 3
    high = lax.Precision.HIGHEST
    cosine, sine = tables[:, :hd], tables[:, hd:]

    def rotate(x):
        return x * cosine + pltpu.roll(x, hd // 2, 1) * sine

    def rotate_back(x):
        return x * cosine - pltpu.roll(x, hd // 2, 1) * sine

    query = rotate(projected[:, :hd].astype(F32))
    keys = rotate(projected[:, hd : 2 * hd].astype(F32))
    values = projected[:, 2 * hd :]
    scale = hd ** (-0.5)
    scores = dot(query, keys, ((1,), (1,)), high) * scale
    scores = jnp.where(allowed, scores, -1e30)
    expo = jnp.exp(scores - jnp.max(scores, axis=1, keepdims=True))
    probs = expo / jnp.sum(expo, axis=1, keepdims=True)
    probs_low = probs.astype(BF16)
    grad_values = dot(probs_low, out_grad, ((0,), (0,)))
    grad_probs = dot(out_grad, values, ((1,), (1,)))
    inner = jnp.sum(grad_probs * probs, axis=1, keepdims=True)
    grad_scores = probs * (grad_probs - inner) * scale
    grad_query = rotate_back(dot(grad_scores, keys, ((1,), (0,)), high))
    grad_keys = rotate_back(dot(grad_scores, query, ((0,), (0,)), high))
    return grad_query.astype(BF16), grad_keys.astype(BF16), grad_values.astype(BF16)


def kernel(
    bit, hops,
    step_ref, doc_ref, tab_ref, act_hbm, w_hbm, first_hbm, second_hbm, og_hbm,
    out_ref,
    act_v, keep, to_pair, to_cross, to_sib, xt, wall, mask, pacc, rec, psend, pz, g_ref,
    tsend, trecv, first_v, second_v, og_v, tacc, t_own, upd, prt,
    loc_sem, w_sem, x_send, x_recv, p_send, p_recv, g_send, g_recv, rs_send, rs_recv, sw_send, sw_recv,
):
    rep = lax.axis_index("rep")
    own = lax.axis_index("fsdp")
    z, core = own // 2, own % 2
    step = 1 - 2 * ((z + core) % 2)
    z_pair, z_next, z_far = (z + step + hops) % hops, (z - step + hops) % hops, (z + 2) % hops
    pair = (rep, z_pair * 2 + core)
    pair_cross = (rep, z_pair * 2 + 1 - core)
    following = (rep, z_next * 2 + core)
    next_cross = (rep, z_next * 2 + 1 - core)
    sibling = (rep, z * 2 + (1 - core))
    distance = 2**bit
    partner = (rep + (1 - 2 * ((rep // distance) % 2)) * distance, own)
    seq, width = act_v.shape
    depth, cols = wall.shape[1:]
    hd = cols // 3
    chunks = depth // CHUNK

    def remote(src, dst, send, recv, device):
        return pltpu.make_async_remote_copy(
            src_ref=src, dst_ref=dst, send_sem=send, recv_sem=recv, device_id=device, device_id_type=MESH
        )

    load_act = pltpu.make_async_copy(act_hbm, act_v, loc_sem.at[0])
    load_w = pltpu.make_async_copy(w_hbm, wall.at[0], loc_sem.at[1])
    load_first = pltpu.make_async_copy(first_hbm, first_v, loc_sem.at[2])
    load_second = pltpu.make_async_copy(second_hbm, second_v, loc_sem.at[3])
    load_og = pltpu.make_async_copy(og_hbm, og_v, loc_sem.at[4])
    for load in (load_act, load_w, load_first, load_second, load_og):
        load.start()

    barrier = pltpu.get_barrier_semaphore()
    greeted = (pair, pair_cross, following, next_cross, sibling, partner)
    for device in greeted:
        pl.semaphore_signal(barrier, inc=1, device_id=device, device_id_type=MESH)
    pl.semaphore_wait(barrier, len(greeted))

    send_w = remote(w_hbm, wall.at[1], w_sem.at[0], w_sem.at[1], following)
    send_w.start()

    load_act.wait()
    piece = seq // PIECES

    def rows_at(base, c):
        return pl.ds(pl.multiple_of(base + c * piece, 16), piece)

    def trade(n, c):
        src, base, device = ((to_pair, 2 * seq, pair), (to_cross, 3 * seq, next_cross), (to_sib, seq, sibling))[n]
        return remote(src.at[:, rows_at(0, c)], keep.at[:, rows_at(base, c)], x_send.at[n, c], x_recv.at[n, c], device)

    places = (
        (z_pair, core, to_pair, 0), (z_far, core, to_pair, 1),
        (z_next, 1 - core, to_cross, 0), (z_far, 1 - core, to_cross, 1),
        (z, 1 - core, to_sib, 0), (z_pair, 1 - core, to_sib, 1),
        (z, core, keep, 0), (z_next, core, keep, 1),
    )

    def norm_piece(c, carry):
        def norm_rows(i, inner):
            rows = pl.ds(pl.multiple_of(c * piece + i * NORM_ROWS, 16), NORM_ROWS)
            values = act_v[rows, :].astype(F32)
            scale = lax.rsqrt(jnp.sum(values * values, axis=-1, keepdims=True) * (1.0 / width) + 1e-05)
            for chip, which, ref, slot in places:
                block = pl.ds(pl.multiple_of((chip * 2 + which) * depth, 128), depth)
                ref[slot, rows, :] = (act_v[rows, block].astype(F32) * scale).astype(BF16)
            return inner

        lax.fori_loop(0, piece // NORM_ROWS, norm_rows, 0)
        for n in range(3):
            trade(n, c).start()
        return carry

    lax.fori_loop(0, PIECES, norm_piece, 0)

    rows = lax.broadcasted_iota(jnp.int32, (seq, seq), 0)
    columns = lax.broadcasted_iota(jnp.int32, (seq, seq), 1)
    doc_wide = jnp.broadcast_to(doc_ref[...].astype(F32), (seq, seq))
    doc_col = jnp.sum(jnp.where(rows == columns, doc_wide, 0.0), axis=1, keepdims=True)
    mask[...] = jnp.where((columns <= rows) & (doc_wide == doc_col), 1.0, 0.0)

    for c in range(PIECES):
        trade(2, c).wait_recv()

    def turn(base):
        for slot in (0, 1):
            xt[slot, :, base : base + 2 * seq] = keep[slot, base : base + 2 * seq, :].T

    turn(0)
    load_w.wait()
    send_w.wait_recv()
    plain = ((1,), (0,))

    def project(base, count):
        part = pl.ds(base, count)
        return dot(keep[0, part, :], wall[0], plain) + dot(keep[1, part, :], wall[1], plain)

    pacc[...] = project(0, 2 * seq)
    give = remote(pacc.at[pl.ds(seq, seq)], rec, p_send.at[0], p_recv.at[0], sibling)
    give.start()
    backs = [
        remote(psend.at[n], pz.at[n], p_send.at[1 + n], p_recv.at[1 + n], device)
        for n, device in enumerate((pair, pair_cross))
    ]
    for n in (0, 1):
        for c in range(PIECES):
            trade(n, c).wait_recv()
        psend[n] = project((2 + n) * seq, seq).astype(BF16)
        backs[n].start()
    turn(2 * seq)
    load_og.wait()
    give.wait_recv()
    for copy in backs:
        copy.wait_recv()
    projected = (pacc[:seq, :] + rec[...] + pz[0].astype(F32) + pz[1].astype(F32)).astype(BF16)
    grads = attention_grad(projected, mask[...] > 0.5, tab_ref[...], og_v[...])
    for n, grad_part in enumerate(grads):
        g_ref[:seq, n * hd : (n + 1) * hd] = grad_part

    g_copies = [
        remote(g_ref.at[pl.ds(0, seq)], g_ref.at[pl.ds(base * seq, seq)], g_send.at[n], g_recv.at[n], device)
        for n, (base, device) in enumerate(((2, pair), (3, next_cross), (1, sibling)))
    ]
    for copy in g_copies:
        copy.start()
    g_copies[2].wait_recv()
    near, far = slice(0, 2 * seq), slice(2 * seq, 4 * seq)
    for slot in (0, 1):
        tacc[slot] = dot(xt[slot, :, near], g_ref[near, :], plain)
    for copy in g_copies[:2]:
        copy.wait_recv()

    def rows_of(i):
        return pl.ds(pl.multiple_of(i * CHUNK, 16), CHUNK)

    def rs_copy(i):
        return remote(tsend.at[rows_of(i)], trecv.at[rows_of(i)], rs_send.at[i], rs_recv.at[i], following)

    def swap_copy(i):
        return remote(upd.at[rows_of(i)], prt.at[rows_of(i)], sw_send.at[i], sw_recv.at[i], partner)

    for start, size in ((0, AHEAD * CHUNK), (AHEAD * CHUNK, depth - AHEAD * CHUNK)):
        part = pl.ds(start, size)
        tsend[part, :] = (tacc[1, part, :] + dot(xt[1, part, far], g_ref[far, :], plain)).astype(BF16)
        if start == 0:
            for i in range(AHEAD):
                rs_copy(i).start()
    t_own[...] = tacc[0] + dot(xt[0, :, far], g_ref[far, :], plain)
    load_first.wait()
    load_second.wait()
    count = jnp.full((1, cols), step_ref[0] + 1, jnp.int32).astype(F32)
    fix_one = 1.0 - jnp.exp(count * LOG_ONE)
    fix_two = 1.0 - jnp.exp(count * LOG_TWO)

    def update(i):
        rows = rows_of(i)
        rs_copy(i).wait_recv()
        grad = t_own[rows, :] + trecv[rows, :].astype(F32)
        weights = wall[0, rows, :].astype(F32)
        first_new = BETA_ONE * first_v[rows, :].astype(F32) + (1.0 - BETA_ONE) * grad
        second_new = BETA_TWO * second_v[rows, :].astype(F32) + (1.0 - BETA_TWO) * grad * grad
        first_hat = first_new / fix_one
        second_hat = second_new / fix_two
        updated = weights - LEARN_RATE * (first_hat / (jnp.sqrt(second_hat) + ADAM_EPS) + DECAY_RATE * weights)
        upd[rows, :] = updated.astype(BF16)
        swap_copy(i).start()
        out_ref[1, rows, :] = first_new.astype(BF16)
        out_ref[2, rows, :] = second_new.astype(BF16)

    def mix(i):
        rows = rows_of(i)
        swap_copy(i).wait_recv()
        out_ref[0, rows, :] = ((upd[rows, :].astype(F32) + prt[rows, :].astype(F32)) * 0.5).astype(BF16)

    def stage(i, carry):
        @pl.when(i < chunks - AHEAD)
        def _():
            rs_copy(i).wait_send()
            rs_copy(i + AHEAD).start()

        @pl.when((i >= LAG) & (i < chunks + LAG))
        def _():
            update(i - LAG)

        @pl.when(i >= LAG + MIX_LAG)
        def _():
            mix(i - LAG - MIX_LAG)

        return carry

    lax.fori_loop(0, chunks + LAG + MIX_LAG, stage, 0)

    for copy in [send_w, give] + backs + g_copies:
        copy.wait_send()
    for c in range(PIECES):
        for n in range(3):
            trade(n, c).wait_send()
    for i in range(chunks - AHEAD, chunks):
        rs_copy(i).wait_send()
    for i in range(chunks):
        swap_copy(i).wait_send()


def per_device(activations, doc_ids, step_index, proj_weights, first_moment, second_moment, out_grad):
    hops = lax.axis_size("fsdp") // 2
    seq, width = activations.shape[1:]
    depth, cols = proj_weights.shape[1:]
    tables = jnp.asarray(rotary_tables(seq, cols // 3))
    dma, vmem = pltpu.SemaphoreType.DMA, pltpu.VMEM
    stages = depth // CHUNK
    row_vmem = vmem((depth, cols), BF16)

    def branch(bit):
        return pl.pallas_call(
            functools.partial(kernel, bit, hops),
            out_shape=jax.ShapeDtypeStruct((3, depth, cols), BF16),
            in_specs=[
                pl.BlockSpec(memory_space=pltpu.SMEM),
                pl.BlockSpec(memory_space=pltpu.VMEM),
                pl.BlockSpec(memory_space=pltpu.VMEM),
            ]
            + [pl.BlockSpec(memory_space=pl.ANY)] * 5,
            out_specs=pl.BlockSpec(memory_space=pltpu.VMEM),
            scratch_shapes=[
                vmem((seq, width), BF16),
                vmem((2, 4 * seq, depth), BF16),
                vmem((2, seq, depth), BF16),
                vmem((2, seq, depth), BF16),
                vmem((2, seq, depth), BF16),
                vmem((2, depth, 4 * seq), BF16),
                vmem((2, depth, cols), BF16),
                vmem((seq, seq), F32),
                vmem((2 * seq, cols), F32),
                vmem((seq, cols), F32),
                vmem((2, seq, cols), BF16),
                vmem((2, seq, cols), BF16),
                vmem((4 * seq, cols), BF16),
                row_vmem,
                row_vmem,
                row_vmem,
                row_vmem,
                vmem((seq, cols // 3), BF16),
                vmem((2, depth, cols), F32),
                vmem((depth, cols), F32),
                row_vmem,
                row_vmem,
                dma((5,)),
                dma((2,)),
                dma((3, PIECES)),
                dma((3, PIECES)),
                dma((3,)),
                dma((3,)),
                dma((3,)),
                dma((3,)),
                dma((stages,)),
                dma((stages,)),
                dma((stages,)),
                dma((stages,)),
            ],
            compiler_params=pltpu.CompilerParams(
                collective_id=bit, has_side_effects=True, vmem_limit_bytes=40 * 2**20
            ),
        )

    bit_total = lax.axis_size("rep").bit_length() - 1
    outs = lax.switch(
        lax.rem(step_index[0], bit_total),
        [branch(bit) for bit in range(bit_total)],
        step_index, doc_ids, tables, activations[0], proj_weights[0], first_moment[0], second_moment[0], out_grad[0],
    )
    return tuple(outs[n : n + 1] for n in range(3))


def solution(mesh):
    rows = P("rep", "fsdp", None)
    return jax.shard_map(
        per_device,
        mesh=mesh,
        in_specs=(rows, P("rep", "fsdp"), P(), rows, rows, rows, rows),
        out_specs=(rows, rows, rows),
        check_vma=False,
    )
```
